128 devices in a mesh: pairs: 32 (over x, z, core), ga: 4 (over y).
Axes of the slice: x: 4, y: 4, z: 4, core: 2. Of those that a mesh axis runs over, the one named last changes fastest.
Arguments:
- densities: bfloat16 [8192, 12000], P('pairs', 'ga'), may hold values from -0.0546875 to 0.0546875
- coulomb: float32 [12000], P('ga'), may hold values from 0.1 to 10
- pair_list: int32 [64, 2], replicated, may hold values from 0 to 7, as said below
- owner: int32 [64, 1], replicated, may hold values from 0 to 31; in each aligned block of 64 rows (0 to 63, 64 to 127, ...) at most 4 rows name the same one
Outputs:
- kernel: float32 [128, 1024, 1024], P('pairs', 'ga')
The draws below stay inside these ranges and needn't reach their ends.
Inputs may be any that keep to these rules, and one draw needn't show every extreme that they name: `pair_list`: each row is a tile pair I <= J; rows are ordered by J - I, never falling. No owner holds more than 4 entries; some owner holds exactly 4.
All inputs are finite; a program needn't handle non-finite values.
Results may differ from the reference program's by a relative error of at most 0.0026.
Values may be sent and summed in bfloat16 or wider, within the bound.
No kernel may reach another device: no remote copies, remote signals or barrier semaphores. Data moves between devices by JAX's collectives and lax.ppermute only.
A program may use at most 192 MiB of HBM per device.

```python
import math
import jax
import jax.numpy as jnp
import numpy as np
from jax import lax

GV = 12000
TILE = 1024
CAP = 4
TRANS = 8192
TILES = 8
NPAIR = 64
SLOTS = 128
N_PAIRS = 32


def draw_pair_list(key, part):
    key = jax.random.fold_in(key, 11)
    key_first, key_second = jax.random.split(key)
    first = jax.random.randint(key_first, (NPAIR,), 0, TILES)
    second = jax.random.randint(key_second, (NPAIR,), 0, TILES)
    lower = jnp.minimum(first, second).at[0].set(0)
    upper = jnp.maximum(first, second).at[0].set(TILES - 1)
    score = (upper - lower) * NPAIR + jnp.arange(NPAIR)
    order = jnp.argsort(score)
    return jnp.stack([lower[order], upper[order]], 1).astype(jnp.int32)


def block_levels(rng, extent, shards, low, high):
    def one(axis_at, parts):
        draws = jax.random.uniform(jax.random.fold_in(jax.random.fold_in(rng, 6), axis_at), (parts,), jnp.float32, low / len(shards), high / len(shards))
        return jnp.repeat(jnp.exp(draws), extent[axis_at] // parts).reshape((-1,) + (1,) * (len(extent) - axis_at - 1))

    factor_of = one(*shards[0])
    for cut in shards[1:]:
        factor_of = factor_of * one(*cut)
    return factor_of


def shared_out(rng, own, number, rows, number_of, top, most, lean):
    ranking = jax.random.permutation(rng, number_of)
    packed, common = load_shares(number_of, rows * top, most, lean, True), load_shares(number_of, rows * top, most, lean, False)
    places = jnp.arange(number_of)

    def named(tallies, turn):
        used = int((tallies > 0).sum())
        fixed = max(1, used // 4)
        shifted = fixed + (places - fixed + turn * (used - fixed)) % max(1, number_of - fixed)
        return jnp.zeros((number_of,), jnp.int32).at[ranking[jnp.where(places < fixed, places, shifted)]].set(jnp.asarray(tallies, jnp.int32))

    tallies = jnp.where(number % 4 == 0, named(packed, number // 4), named(common, number - number // 4 - 1))
    mixed = jax.random.permutation(jax.random.fold_in(own, 3), number_of)
    donor, taker = mixed[0:number_of // 2 * 2:2], mixed[1:number_of // 2 * 2:2]
    margin = jnp.minimum(tallies[donor] - 1, most - tallies[taker]) // 2
    margin = jnp.where((donor == ranking[0]) | (taker == ranking[0]) | (tallies[taker] == 0), 0, jnp.maximum(margin, 0))
    shifted = jax.random.randint(jax.random.fold_in(own, 4), (number_of // 2,), 0, 1 << 20) % (margin + 1)
    tallies = tallies.at[donor].add(-shifted).at[taker].add(shifted)
    items = jnp.searchsorted(jnp.cumsum(tallies), jnp.arange(rows * top), side="right").astype(jnp.int32)
    grid = items.reshape(top, rows).T
    grid = grid[jax.random.permutation(jax.random.fold_in(own, 1), rows)]
    turn = jax.random.randint(jax.random.fold_in(own, 2), (rows, 1), 0, top)
    return jnp.take_along_axis(grid, (jnp.arange(top)[None, :] + turn) % top, axis=1)


def load_shares(number_of, total, limit, skew, full):
    portions = [(1 << 20) // math.isqrt(rank ** skew) + 1 for rank in range(1, number_of + 1)]
    largest = limit if full else min(limit, max(-(-total // number_of), total * portions[0] // sum(portions)))
    least = 1 if total - largest >= number_of - 1 else 0
    holding, surplus = [largest] + [least] * (number_of - 1), total - largest - least * (number_of - 1)
    while surplus > 0:
        free = [i for i in range(1, number_of) if holding[i] < largest] or [i for i in range(1, number_of) if holding[i] < limit]
        pool, remaining = sum([portions[i] for i in free]), surplus
        for i in free:
            addition = min(limit - holding[i], max(1, remaining * portions[i] // pool), surplus)
            holding[i] = holding[i] + addition
            surplus = surplus - addition
    return np.array(holding)


def centred(rng, extent, deviation, most, cuts=(), kind=jnp.bfloat16):
    drawn = deviation * jax.random.normal(rng, extent, jnp.float32)
    if cuts:
        drawn = drawn * block_levels(rng, extent, cuts, -0.22, 0.18)
    return jnp.clip(drawn, -most, most).astype(kind)


def setup_inputs(seed: int = 0) -> dict:
    seeds = jax.random.split(jax.random.key(seed), 5)
    densities = centred(seeds[0], (TRANS, GV), (GV ** -0.5), 0.0546875, ((0, 32), (1, 4)))
    coulomb = jnp.clip(jnp.exp(math.log(10.0) - 4.6051702 * jax.random.uniform(seeds[1], (GV,), jnp.float32) ** block_levels(seeds[1], (GV,), ((0, 4),), -0.2, 0.2)), 0.1, 10.0)
    pair_list = draw_pair_list(jax.random.fold_in(seeds[4], 71), 0)
    owner_keys = jax.random.split(jax.random.fold_in(seeds[3], 1), NPAIR // NPAIR)
    owner_turns = jax.random.permutation(jax.random.fold_in(seeds[3], 3), NPAIR // NPAIR)
    owner = jax.vmap(lambda own, number: shared_out(jax.random.fold_in(seeds[3], 2), own, number, NPAIR, N_PAIRS, 1, CAP, 2))(owner_keys, owner_turns).reshape((NPAIR, 1))
    return dict(densities=densities, coulomb=coulomb, pair_list=pair_list, owner=owner)


def reference(densities, coulomb, pair_list, owner):
    weighted = (densities.astype(jnp.float32) * coulomb[None, :]).astype(jnp.bfloat16)
    owner_ids = owner[:, 0]
    onehot = (owner_ids[:, None] == jnp.arange(N_PAIRS, dtype=jnp.int32)[None, :]).astype(jnp.int32)
    rank = jnp.sum((jnp.cumsum(onehot, 0) - onehot) * onehot, 1).astype(jnp.int32)
    slot = (owner_ids * CAP + rank).astype(jnp.int32)

    def single(pair):
        left = lax.dynamic_slice_in_dim(weighted, (pair[0] * TILE).astype(jnp.int32), TILE, 0)
        right = lax.dynamic_slice_in_dim(densities, (pair[1] * TILE).astype(jnp.int32), TILE, 0)
        return jnp.dot(left, right.T, preferred_element_type=jnp.float32)

    grams = lax.map(single, pair_list)
    return jnp.zeros((SLOTS, TILE, TILE), jnp.float32).at[slot].set(grams)
```

```python
import jax
import jax.numpy as jnp
from jax import lax
from jax.experimental import pallas as pl
from jax.experimental.pallas import tpu as pltpu
from jax.sharding import Mesh
from jax.sharding import PartitionSpec as P

TILES = 8
CAP = 4
NP = TILES * (TILES + 1) // 2
BF = jnp.bfloat16
F32 = jnp.float32
STEPS = [(i, j) for j in range(4) for i in range(j + 1)]
MIB = 1 << 20


def shift(a, axis, d):
    return lax.ppermute(a, axis, [(i, (i + d) % 4) for i in range(4)])


def gather4(a, axis):
    half = a.shape[0] // 2
    low, high = shift(a, axis, 1), shift(a, axis, -1)
    far0 = shift(low[:half], axis, 1)
    far1 = shift(high[half:], axis, -1)
    return a, high, far0, far1, low


def gram_kernel(meta, steps_i, steps_j, *refs):
    lefts, rights = refs[:10], refs[10:20]
    own, s1, s2, s3 = refs[20:24]
    lbuf, rbuf, sems = refs[24:]
    x, z, c, y = meta[0], meta[1], meta[2], meta[3]
    copies = []

    def copy(src, dst):
        copies.append(pltpu.make_async_copy(src, dst, sems.at[len(copies)]))
        copies[-1].start()

    for half in range(2):
        parity = (z // 2 + half) % 2
        mine = rights[5 * half : 5 * half + 5]
        for dx, ref, lo in ((0, mine[0], 0), (1, mine[1], 0), (2, mine[2], 0), (2, mine[3], 64), (3, mine[4], 0)):
            tile = 2 * ((x + dx) % 4) + parity
            copy(ref, rbuf.at[tile, pl.ds(lo, ref.shape[0])])
    for dc in range(2):
        mine = lefts[5 * dc : 5 * dc + 5]
        for dz, ref, first in ((0, mine[0], 0), (1, mine[1], 0), (2, mine[2], 0), (2, mine[3], 2), (3, mine[4], 0)):
            zz = (z + dz) % 4
            quarter = 2 * (zz % 2) + (c + dc) % 2
            for k in range(ref.shape[0]):
                tile = 2 * ((x + first + k) % 4) + zz // 2
                copy(ref.at[k], lbuf.at[tile, (quarter - y + 4) % 4])
    for item in copies:
        item.wait()

    def step(t, _):
        ip, jp = steps_i[t], steps_j[t]
        left = lbuf[pl.ds(2 * ip, 2)].reshape(512, lbuf.shape[-1])
        right = rbuf[pl.ds(2 * jp, 2)].reshape(256, rbuf.shape[-1])
        out = lax.dot_general(left, right, (((1,), (1,)), ((), ())), preferred_element_type=F32)
        for a in range(2):
            for b in range(2):
                i, j = 2 * ip + a, 2 * jp + b

                @pl.when(i <= j)
                def _():
                    at = j * (j + 1) // 2 + i
                    part = out[256 * a : 256 * a + 256, 128 * b : 128 * b + 128]
                    own[at] = part[0:64]
                    s1[at] = part[64:128].astype(BF)
                    s2[at] = part[128:192].astype(BF)
                    s3[at] = part[192:256].astype(BF)

        return 0

    lax.fori_loop(0, len(STEPS), step, 0)


def grams(meta, lefts, rights):
    width = rights[0].shape[-1]
    any_ = pl.BlockSpec(memory_space=pl.ANY)
    smem = pl.BlockSpec(memory_space=pltpu.SMEM)
    vmem = pl.BlockSpec(memory_space=pltpu.VMEM)
    piece = (NP, 64, 128)
    return pl.pallas_call(
        gram_kernel,
        out_shape=[jax.ShapeDtypeStruct(piece, F32)] + [jax.ShapeDtypeStruct(piece, BF)] * 3,
        in_specs=[smem] * 3 + [any_] * 20,
        out_specs=[vmem] * 4,
        scratch_shapes=[
            pltpu.VMEM((TILES, 4, 64, width), BF),
            pltpu.VMEM((TILES, 128, width), BF),
            pltpu.SemaphoreType.DMA((42,)),
        ],
        compiler_params=pltpu.CompilerParams(vmem_limit_bytes=48 * MIB),
        cost_estimate=pl.CostEstimate(
            flops=2 * 10 * 512 * 256 * width, bytes_accessed=20 * MIB, transcendentals=0
        ),
        name="grams",
    )(
        meta,
        jnp.array([s[0] for s in STEPS], jnp.int32),
        jnp.array([s[1] for s in STEPS], jnp.int32),
        *lefts,
        *rights,
    )


def route_kernel(index, valid, own, a, b, c, out, total):
    total[...] = (
        own[...] + a[...].astype(F32) + b[...].astype(F32) + c[...].astype(F32)
    ).astype(BF)

    def one(k, _):
        @pl.when(valid[k] > 0)
        def _():
            out[k] = total[index[k]]

        @pl.when(valid[k] == 0)
        def _():
            out[k] = jnp.zeros(out.shape[1:], BF)

        return 0

    lax.fori_loop(0, out.shape[0], one, 0)


def route(index, valid, own, parts):
    smem = pl.BlockSpec(memory_space=pltpu.SMEM)
    vmem = pl.BlockSpec(memory_space=pltpu.VMEM)
    return pl.pallas_call(
        route_kernel,
        out_shape=jax.ShapeDtypeStruct((index.shape[0], 64, 128), BF),
        in_specs=[smem, smem] + [vmem] * 4,
        out_specs=vmem,
        scratch_shapes=[pltpu.VMEM((NP, 64, 128), BF)],
        compiler_params=pltpu.CompilerParams(vmem_limit_bytes=32 * MIB),
        name="route",
    )(index, valid, own, *parts)


def place_kernel(got, out):
    for src in range(32):
        x, z1, z0, c = src // 8, (src // 4) % 2, (src // 2) % 2, src % 2
        col = (4 * z0 + 2 * c + z1) * 128
        for h in range(2):
            row = h * 128 + x * 32
            out[0, row : row + 32, col : col + 128] = got[src, 0, 32 * h : 32 * h + 32].astype(F32)


def place(got):
    return pl.pallas_call(
        place_kernel,
        grid=(CAP,),
        out_shape=jax.ShapeDtypeStruct((CAP, 256, 1024), F32),
        in_specs=[pl.BlockSpec((32, 1, 64, 128), lambda s: (0, s, 0, 0))],
        out_specs=pl.BlockSpec((1, 256, 1024), lambda s: (s, 0, 0)),
        name="place",
    )(got)


def on_device(densities, coulomb, pair_list, owner):
    x, z, c, y = (lax.axis_index(n) for n in ("x", "z", "c", "y"))
    z1 = z // 2
    rows, k = densities.shape
    width = -(-k // 128) * 128
    dens = jnp.pad(densities, ((0, 0), (0, width - k)))
    weights = jnp.pad(coulomb, (0, width - k))

    keep = lax.dynamic_slice_in_dim(dens, z1 * 128, 128, 0)
    send = lax.dynamic_slice_in_dim(dens, (1 - z1) * 128, 128, 0)
    got = shift(send, "z", 2)

    quarter = dens.reshape(2, 4, 32, width)

    def weighted_part(to):
        part = lax.dynamic_slice_in_dim(quarter, to, 1, 1).reshape(1, 64, width)
        return (part.astype(F32) * weights).astype(BF)

    mine = [weighted_part(lax.rem(x + d, 4)) for d in range(4)]
    left = jnp.concatenate(
        [mine[0], shift(mine[3], "x", 3), shift(mine[2], "x", 2), shift(mine[1], "x", 1)], 0
    )
    rights = gather4(keep, "x") + gather4(got, "x")
    lefts = gather4(left, "z")
    lefts = lefts + tuple(lax.ppermute(a, "c", [(0, 1), (1, 0)]) for a in lefts)
    meta = jnp.stack([x, z, c, y]).astype(jnp.int32)
    own, s1, s2, s3 = grams(meta, lefts, rights)
    parts = [shift(s1, "y", 1), shift(s2, "y", 2), shift(s3, "y", 3)]

    owners = 32
    owner_ids = owner[:, 0]
    onehot = (owner_ids[:, None] == jnp.arange(owners, dtype=jnp.int32)[None, :]).astype(jnp.int32)
    rank = jnp.sum((jnp.cumsum(onehot, 0) - onehot) * onehot, 1)
    slot = owner_ids * CAP + rank
    match = (slot[None, :] == jnp.arange(owners * CAP, dtype=jnp.int32)[:, None]).astype(jnp.int32)
    second = pair_list[:, 1]
    which = second * (second + 1) // 2 + pair_list[:, 0]
    index = jnp.sum(match * which[None, :], 1)
    valid = jnp.sum(match, 1)

    routed = route(index, valid, own, parts).reshape(owners, CAP, 64, 128)
    arrived = lax.all_to_all(routed, ("x", "z", "c"), 0, 0, tiled=True)
    return place(arrived)


def solution(mesh):
    grid = Mesh(mesh.devices.reshape(4, 4, 2, 4), ("x", "z", "c", "y"))
    pairs = ("x", "z", "c")
    return jax.shard_map(
        on_device,
        mesh=grid,
        in_specs=(P(pairs, "y"), P("y"), P(), P()),
        out_specs=P(pairs, "y", None),
        check_vma=False,
    )
```

```python
import jax
import jax.numpy as jnp
from jax import lax
from jax.experimental import pallas as pl
from jax.experimental.pallas import tpu as pltpu
from jax.sharding import Mesh
from jax.sharding import PartitionSpec as P

TILES = 8
CAP = 4
NP = TILES * (TILES + 1) // 2
BF = jnp.bfloat16
F32 = jnp.float32
MIB = 1 << 20


def shift(a, axis, d):
    return lax.ppermute(a, axis, [(i, (i + d) % 4) for i in range(4)])


def tie(*arrays):
    return lax.optimization_barrier(arrays)


def left_slot(z, c, zz, cc):
    own = zz // 2 == z // 2
    near = jnp.where(zz % 2 == z % 2, 6, 4) + cc
    return jnp.where(own, 2 * (zz % 2) + cc, near)


def load(meta, lefts, rights, lbuf, rbuf, sems):
    x, z, c = meta[0], meta[1], meta[2]
    copies = []

    def copy(src, dst):
        copies.append(pltpu.make_async_copy(src, dst, sems.at[len(copies)]))
        copies[-1].start()

    for (half, dx), ref in rights:
        copy(ref, rbuf.at[(x + dx) % 4, (z // 2 + half) % 2])
    for (dc, dz, first), ref in lefts:
        zz = (z + dz) % 4
        slot = left_slot(z, c, zz, (c + dc) % 2)
        for k in range(ref.shape[0]):
            copy(ref.at[k], lbuf.at[(x + first + k) % 4, slot])
    for item in copies:
        item.wait()


def product(left, right):
    return lax.dot_general(left, right, (((1,), (1,)), ((), ())), preferred_element_type=F32)


def store(meta, outs, part, i, j, slot_quarter):
    dy = (slot_quarter - meta[3] + 4) % 4
    at = j * (j + 1) // 2 + i
    for k in range(4):

        @pl.when((i <= j) & (dy == k))
        def _():
            outs[k][at] = part.astype(outs[k].dtype)


def store_slots(meta, outs, out, ip, jp, slots, row):
    z = meta[1]
    z1, z0 = z // 2, z % 2
    for n, slot in enumerate(slots):
        if slot < 4:
            i, quarter = 2 * ip + z1, slot
        elif slot < 6:
            i, quarter = 2 * ip + 1 - z1, 2 * (1 - z0) + slot - 4
        else:
            i, quarter = 2 * ip + 1 - z1, 2 * z0 + slot - 6
        for b in range(2):
            part = out[row + 64 * n : row + 64 * n + 64, 128 * b : 128 * b + 128]
            store(meta, outs, part, i, 2 * jp + b, quarter)


EARLY_L = [(dc, dz, 0) for dc in range(2) for dz in (0, 1, 3)]
LATE_L = [(dc, 2, first) for dc in range(2) for first in (0, 2)]
EARLY_R = [(half, dx) for half in range(2) for dx in (0, 1, 3)]
LATE_R = [(half, 2) for half in range(2)]


def early_kernel(meta, *refs):
    n = len(EARLY_L) + len(EARLY_R)
    lefts = list(zip(EARLY_L, refs))
    rights = list(zip(EARLY_R, refs[len(EARLY_L) :]))
    outs, (lbuf, rbuf, sems) = refs[n : n + 4], refs[n + 4 :]
    load(meta, lefts, rights, lbuf, rbuf, sems)
    x = meta[0]
    width = lbuf.shape[-1]

    for dx in (0, 1, 3):
        jp = (x + dx) % 4

        def step(ip, _):
            out = product(lbuf[ip].reshape(384, width), rbuf[jp].reshape(256, width))
            store_slots(meta, outs, out, ip, jp, range(6), 0)
            return 0

        lax.fori_loop(0, jp + 1, step, 0)


def late_kernel(meta, *refs):
    keys_l, keys_r = EARLY_L + LATE_L, EARLY_R + LATE_R
    n = len(keys_l) + len(keys_r)
    lefts = list(zip(keys_l, refs))
    rights = list(zip(keys_r, refs[len(keys_l) :]))
    done, outs = refs[n : n + 4], refs[n + 4 : n + 8]
    lbuf, rbuf, sems = refs[n + 8 :]
    for a, b in zip(done, outs):
        b[...] = a[...]
    load(meta, lefts, rights, lbuf, rbuf, sems)
    x = meta[0]
    width = lbuf.shape[-1]

    def near(k, _):
        jp = (x + jnp.where(k == 2, 3, k)) % 4
        left = lbuf[:, 6:8].reshape(512, width)
        out = product(left, rbuf[jp].reshape(256, width))
        for ip in range(4):
            store_slots(meta, outs, out, ip, jp, (6, 7), 128 * ip)
        return 0

    lax.fori_loop(0, 3, near, 0)
    jp = (x + 2) % 4

    def far(ip, _):
        out = product(lbuf[ip].reshape(512, width), rbuf[jp].reshape(256, width))
        store_slots(meta, outs, out, ip, jp, range(8), 0)
        return 0

    lax.fori_loop(0, jp + 1, far, 0)


def grams(meta, lefts, rights, done):
    width = rights[0].shape[-1]
    any_ = pl.BlockSpec(memory_space=pl.ANY)
    smem = pl.BlockSpec(memory_space=pltpu.SMEM)
    vmem = pl.BlockSpec(memory_space=pltpu.VMEM)
    piece = (NP, 64, 128)
    slots = 8 if done else 6
    return pl.pallas_call(
        late_kernel if done else early_kernel,
        out_shape=[jax.ShapeDtypeStruct(piece, F32)] + [jax.ShapeDtypeStruct(piece, BF)] * 3,
        in_specs=[smem] + [any_] * (len(lefts) + len(rights)) + [vmem] * len(done),
        out_specs=[vmem] * 4,
        scratch_shapes=[
            pltpu.VMEM((4, slots, 64, width), BF),
            pltpu.VMEM((4, 2, 128, width), BF),
            pltpu.SemaphoreType.DMA((40,)),
        ],
        compiler_params=pltpu.CompilerParams(vmem_limit_bytes=48 * MIB),
        cost_estimate=pl.CostEstimate(
            flops=2 * 8 * 384 * 256 * width, bytes_accessed=20 * MIB, transcendentals=0
        ),
        name="late_grams" if done else "early_grams",
    )(meta, *lefts, *rights, *done)


def route_kernel(index, valid, own, a, b, c, out, total):
    total[...] = (
        own[...] + a[...].astype(F32) + b[...].astype(F32) + c[...].astype(F32)
    ).astype(BF)

    def one(k, _):
        @pl.when(valid[k] > 0)
        def _():
            out[k] = total[index[k]]

        @pl.when(valid[k] == 0)
        def _():
            out[k] = jnp.zeros(out.shape[1:], BF)

        return 0

    lax.fori_loop(0, out.shape[0], one, 0)


def route(index, valid, own, parts):
    smem = pl.BlockSpec(memory_space=pltpu.SMEM)
    vmem = pl.BlockSpec(memory_space=pltpu.VMEM)
    return pl.pallas_call(
        route_kernel,
        out_shape=jax.ShapeDtypeStruct((index.shape[0], 64, 128), BF),
        in_specs=[smem, smem] + [vmem] * 4,
        out_specs=vmem,
        scratch_shapes=[pltpu.VMEM((NP, 64, 128), BF)],
        compiler_params=pltpu.CompilerParams(vmem_limit_bytes=32 * MIB),
        name="route",
    )(index, valid, own, *parts)


def place_kernel(got, out):
    for src in range(32):
        x, z1, z0, c = src // 8, (src // 4) % 2, (src // 2) % 2, src % 2
        col = (4 * z0 + 2 * c + z1) * 128
        for h in range(2):
            row = h * 128 + x * 32
            out[0, row : row + 32, col : col + 128] = got[src, 0, 32 * h : 32 * h + 32].astype(F32)


def place(got):
    return pl.pallas_call(
        place_kernel,
        grid=(CAP,),
        out_shape=jax.ShapeDtypeStruct((CAP, 256, 1024), F32),
        in_specs=[pl.BlockSpec((32, 1, 64, 128), lambda s: (0, s, 0, 0))],
        out_specs=pl.BlockSpec((1, 256, 1024), lambda s: (s, 0, 0)),
        name="place",
    )(got)


def on_device(densities, coulomb, pair_list, owner):
    x, z, c, y = (lax.axis_index(n) for n in ("x", "z", "c", "y"))
    z1 = z // 2
    rows, k = densities.shape
    width = -(-k // 128) * 128
    dens = jnp.pad(densities, ((0, 0), (0, width - k)))
    weights = jnp.pad(coulomb, (0, width - k))

    keep = lax.dynamic_slice_in_dim(dens, z1 * 128, 128, 0)
    send = lax.dynamic_slice_in_dim(dens, (1 - z1) * 128, 128, 0)
    got = shift(send, "z", 2)

    quarter = dens.reshape(2, 4, 32, width)

    def weighted_part(to):
        part = lax.dynamic_slice_in_dim(quarter, to, 1, 1).reshape(1, 64, width)
        return (part.astype(F32) * weights).astype(BF)

    mine = [weighted_part(lax.rem(x + d, 4)) for d in range(4)]
    other = [(0, 1), (1, 0)]
    got, e1, e2, e3 = tie(
        got, shift(mine[3], "x", 3), shift(mine[2], "x", 2), shift(mine[1], "x", 1)
    )
    left = jnp.concatenate([mine[0], e1, e2, e3], 0)
    keep, got, left = tie(keep, got, left)

    keep3, keep1 = shift(keep, "x", 1), shift(keep, "x", -1)
    got3, got1 = shift(got, "x", 1), shift(got, "x", -1)
    left3, left1 = shift(left, "z", 1), shift(left, "z", -1)
    swap0 = lax.ppermute(left, "c", other)
    keep3, keep1, got3, got1, left3, left1, swap0 = tie(
        keep3, keep1, got3, got1, left3, left1, swap0
    )

    keep2, got2 = shift(keep3, "x", 1), shift(got1, "x", -1)
    left2a, left2b = shift(left3[:2], "z", 1), shift(left1[2:], "z", -1)
    swap1, swap3 = lax.ppermute(left1, "c", other), lax.ppermute(left3, "c", other)
    meta = jnp.stack([x, z, c, y]).astype(jnp.int32)
    lefts = [left, left1, left3, swap0, swap1, swap3]
    rights = [keep, keep1, keep3, got, got1, got3]
    done = grams(meta, lefts, rights, [])
    swap2a, swap2b = lax.ppermute(left2a, "c", other), lax.ppermute(left2b, "c", other)
    own, s1, s2, s3 = grams(
        meta, lefts + [left2a, left2b, swap2a, swap2b], rights + [keep2, got2], done
    )
    parts = [shift(s1, "y", 1), shift(s2, "y", 2), shift(s3, "y", 3)]

    owners = 32
    owner_ids = owner[:, 0]
    onehot = (owner_ids[:, None] == jnp.arange(owners, dtype=jnp.int32)[None, :]).astype(jnp.int32)
    rank = jnp.sum((jnp.cumsum(onehot, 0) - onehot) * onehot, 1)
    slot = owner_ids * CAP + rank
    match = (slot[None, :] == jnp.arange(owners * CAP, dtype=jnp.int32)[:, None]).astype(jnp.int32)
    second = pair_list[:, 1]
    which = second * (second + 1) // 2 + pair_list[:, 0]
    index = jnp.sum(match * which[None, :], 1)
    valid = jnp.sum(match, 1)

    routed = route(index, valid, own, parts).reshape(owners, CAP, 64, 128)
    arrived = lax.all_to_all(routed, ("x", "z", "c"), 0, 0, tiled=True)
    return place(arrived)


def solution(mesh):
    grid = Mesh(mesh.devices.reshape(4, 4, 2, 4), ("x", "z", "c", "y"))
    pairs = ("x", "z", "c")
    return jax.shard_map(
        on_device,
        mesh=grid,
        in_specs=(P(pairs, "y"), P("y"), P(), P()),
        out_specs=P(pairs, "y", None),
        check_vma=False,
    )
```

```python
import jax
import jax.numpy as jnp
from jax import lax
from jax.experimental import pallas as pl
from jax.experimental.pallas import tpu as pltpu
from jax.sharding import Mesh
from jax.sharding import PartitionSpec as P

TILES = 8
CAP = 4
NP = TILES * (TILES + 1) // 2
BF = jnp.bfloat16
F32 = jnp.float32
MIB = 1 << 20


def shift(a, axis, d):
    return lax.ppermute(a, axis, [(i, (i + d) % 4) for i in range(4)])


def tie(*arrays):
    return lax.optimization_barrier(arrays)


EARLY_L = [(dc, dz) for dc in range(2) for dz in (0, 1, 3)]
LATE_L = [(dc, 2) for dc in range(2)]


def product(lefts, rights):
    return lax.dot_general(
        jnp.concatenate(lefts, 0),
        jnp.concatenate(rights, 0),
        (((1,), (1,)), ((), ())),
        preferred_element_type=F32,
    )


def store(meta, sums, out, ip, jp, sources, row):
    z, c, y = meta[1], meta[2], meta[3]
    for n, (dc, dz) in enumerate(sources):
        zz, cc = (z + dz) % 4, (c + dc) % 2
        i = 2 * ip + zz // 2
        dy = (2 * (zz % 2) + cc - y + 4) % 4
        for half in range(2):
            j = 2 * jp + (z // 2 + half) % 2
            at = jnp.where(i <= j, j * (j + 1) // 2 + i, NP)
            sums[dy, at] = out[row + 64 * n : row + 64 * n + 64, 128 * half : 128 * half + 128]


def early_kernel(meta, *refs):
    lefts, rights, sums = refs[:6], refs[6:12], refs[12]
    x = meta[0]
    for n, dx in enumerate((0, 1, 3)):
        jp = (x + dx) % 4
        right = [rights[n], rights[3 + n]]

        def step(k, _):
            ip = (x + k) % 4

            @pl.when(ip <= jp)
            def _():
                out = product([ref[k] for ref in lefts], [ref[...] for ref in right])
                store(meta, sums, out, ip, jp, EARLY_L, 0)

            return 0

        lax.fori_loop(0, 4, step, 0)


def late_kernel(meta, *refs):
    lefts, rights, late, far = refs[:6], refs[6:12], refs[12:16], refs[16:18]
    own, s1, s2, s3, sums = refs[19:24]
    x = meta[0]

    def late_of(k):
        return [late[2 * dc + k // 2][k % 2] for dc in range(2)]

    for n, dx in enumerate((0, 1, 3)):
        jp = (x + dx) % 4
        rows = [block for k in range(4) for block in late_of(k)]
        out = product(rows, [rights[n][...], rights[3 + n][...]])
        for k in range(4):
            store(meta, sums, out, (x + k) % 4, jp, LATE_L, 128 * k)
    jp = (x + 2) % 4
    for k in range(4):
        ip = (x + k) % 4

        @pl.when(ip <= jp)
        def _():
            rows = [ref[k] for ref in lefts] + late_of(k)
            out = product(rows, [ref[...] for ref in far])
            store(meta, sums, out, ip, jp, EARLY_L + LATE_L, 0)

    own[...] = sums[0, :NP]
    for k, ref in enumerate((s1, s2, s3)):
        ref[...] = sums[k + 1, :NP].astype(BF)


def grams(meta, lefts, rights, late=(), far=(), sums=()):
    width = rights[0].shape[-1]
    smem = pl.BlockSpec(memory_space=pltpu.SMEM)
    vmem = pl.BlockSpec(memory_space=pltpu.VMEM)
    piece = (NP, 64, 128)
    given = [*lefts, *rights, *late, *far, *sums]
    shapes = [jax.ShapeDtypeStruct((4, NP + 1, 64, 128), F32)]
    if late:
        shapes = [jax.ShapeDtypeStruct(piece, F32)] + [jax.ShapeDtypeStruct(piece, BF)] * 3 + shapes
    return pl.pallas_call(
        late_kernel if late else early_kernel,
        out_shape=shapes,
        in_specs=[smem] + [vmem] * len(given),
        out_specs=[vmem] * len(shapes),
        input_output_aliases={len(given): 4} if late else {},
        compiler_params=pltpu.CompilerParams(vmem_limit_bytes=16 * MIB),
        cost_estimate=pl.CostEstimate(
            flops=2 * 8 * 384 * 256 * width, bytes_accessed=20 * MIB, transcendentals=0
        ),
        name="late_grams" if late else "early_grams",
    )(meta, *given)


def prepare_kernel(meta, dens, weights, keep, send, *parts):
    k, width = dens.shape[1], keep.shape[1]
    x, z1 = meta[0], meta[1] // 2
    edge = k // 128 * 128
    for ref in (keep, send):
        ref[:, edge:] = jnp.zeros((128, width - edge), BF)
    keep[:, :k] = dens[pl.ds(pl.multiple_of(z1 * 128, 128), 128), :]
    send[:, :k] = dens[pl.ds(pl.multiple_of((1 - z1) * 128, 128), 128), :]
    for d, ref in enumerate(parts):
        ref[0, :, edge:] = jnp.zeros((64, width - edge), BF)
        for h in range(2):
            row = pl.multiple_of(h * 128 + (x + d) % 4 * 32, 32)
            part = dens[pl.ds(row, 32), :].astype(F32) * weights[...]
            ref[0, 32 * h : 32 * h + 32, :k] = part.astype(BF)


def prepare(meta, dens, weights, width):
    smem = pl.BlockSpec(memory_space=pltpu.SMEM)
    vmem = pl.BlockSpec(memory_space=pltpu.VMEM)
    shapes = [jax.ShapeDtypeStruct((128, width), BF)] * 2
    shapes += [jax.ShapeDtypeStruct((1, 64, width), BF)] * 4
    return pl.pallas_call(
        prepare_kernel,
        out_shape=shapes,
        in_specs=[smem, vmem, vmem],
        out_specs=[vmem] * 6,
        compiler_params=pltpu.CompilerParams(vmem_limit_bytes=16 * MIB),
        name="prepare",
    )(meta, dens, weights)


def route_kernel(index, valid, own, a, b, c, out, total):
    total[...] = (
        own[...] + a[...].astype(F32) + b[...].astype(F32) + c[...].astype(F32)
    ).astype(BF)

    def one(k, _):
        @pl.when(valid[k] > 0)
        def _():
            out[k] = total[index[k]]

        @pl.when(valid[k] == 0)
        def _():
            out[k] = jnp.zeros(out.shape[1:], BF)

        return 0

    lax.fori_loop(0, out.shape[0], one, 0)


def route(index, valid, own, parts):
    smem = pl.BlockSpec(memory_space=pltpu.SMEM)
    vmem = pl.BlockSpec(memory_space=pltpu.VMEM)
    return pl.pallas_call(
        route_kernel,
        out_shape=jax.ShapeDtypeStruct((index.shape[0], 64, 128), BF),
        in_specs=[smem, smem] + [vmem] * 4,
        out_specs=vmem,
        scratch_shapes=[pltpu.VMEM((NP, 64, 128), BF)],
        compiler_params=pltpu.CompilerParams(vmem_limit_bytes=32 * MIB),
        name="route",
    )(index, valid, own, *parts)


def place_kernel(got, out):
    for src in range(32):
        x, z1, z0, c = src // 8, (src // 4) % 2, (src // 2) % 2, src % 2
        col = (4 * z0 + 2 * c + z1) * 128
        for h in range(2):
            row = h * 128 + x * 32
            out[0, row : row + 32, col : col + 128] = got[src, 0, 32 * h : 32 * h + 32].astype(F32)


def place(got):
    return pl.pallas_call(
        place_kernel,
        grid=(CAP,),
        out_shape=jax.ShapeDtypeStruct((CAP, 256, 1024), F32),
        in_specs=[pl.BlockSpec((32, 1, 64, 128), lambda s: (0, s, 0, 0))],
        out_specs=pl.BlockSpec((1, 256, 1024), lambda s: (s, 0, 0)),
        name="place",
    )(got)


def on_device(densities, coulomb, pair_list, owner):
    x, z, c, y = (lax.axis_index(n) for n in ("x", "z", "c", "y"))
    k = densities.shape[1]
    meta = jnp.stack([x, z, c, y]).astype(jnp.int32)
    keep, send, *mine = prepare(meta, densities, coulomb[None, :], -(-k // 128) * 128)
    got = shift(send, "z", 2)
    other = [(0, 1), (1, 0)]
    got, e1, e2, e3 = tie(
        got, shift(mine[3], "x", 3), shift(mine[2], "x", 2), shift(mine[1], "x", 1)
    )
    left = jnp.concatenate([mine[0], e1, e2, e3], 0)
    keep, got, left = tie(keep, got, left)

    keep3, keep1 = shift(keep, "x", 1), shift(keep, "x", -1)
    got3, got1 = shift(got, "x", 1), shift(got, "x", -1)
    left3, left1 = shift(left, "z", 1), shift(left, "z", -1)
    swap0 = lax.ppermute(left, "c", other)
    keep3, keep1, got3, got1, left3, left1, swap0 = tie(
        keep3, keep1, got3, got1, left3, left1, swap0
    )

    keep2, got2 = shift(keep3, "x", 1), shift(got1, "x", -1)
    left2a, left2b = shift(left3[:2], "z", 1), shift(left1[2:], "z", -1)
    swap1, swap3 = lax.ppermute(left1, "c", other), lax.ppermute(left3, "c", other)
    lefts = [left, left1, left3, swap0, swap1, swap3]
    rights = [keep, keep1, keep3, got, got1, got3]
    (sums,) = grams(meta, lefts, rights)
    left2a, left2b, sums = tie(left2a, left2b, sums)
    swap2a, swap2b = lax.ppermute(left2a, "c", other), lax.ppermute(left2b, "c", other)
    late = [left2a, left2b, swap2a, swap2b]
    own, s1, s2, s3, _ = grams(meta, lefts, rights, late, [keep2, got2], [sums])
    parts = [shift(s1, "y", 1), shift(s2, "y", 2), shift(s3, "y", 3)]

    owners = 32
    owner_ids = owner[:, 0]
    onehot = (owner_ids[:, None] == jnp.arange(owners, dtype=jnp.int32)[None, :]).astype(jnp.int32)
    rank = jnp.sum((jnp.cumsum(onehot, 0) - onehot) * onehot, 1)
    slot = owner_ids * CAP + rank
    match = (slot[None, :] == jnp.arange(owners * CAP, dtype=jnp.int32)[:, None]).astype(jnp.int32)
    second = pair_list[:, 1]
    which = second * (second + 1) // 2 + pair_list[:, 0]
    index = jnp.sum(match * which[None, :], 1)
    valid = jnp.sum(match, 1)

    routed = route(index, valid, own, parts).reshape(owners, CAP, 64, 128)
    arrived = lax.all_to_all(routed, ("x", "z", "c"), 0, 0, tiled=True)
    return place(arrived)


def solution(mesh):
    grid = Mesh(mesh.devices.reshape(4, 4, 2, 4), ("x", "z", "c", "y"))
    pairs = ("x", "z", "c")
    return jax.shard_map(
        on_device,
        mesh=grid,
        in_specs=(P(pairs, "y"), P("y"), P(), P()),
        out_specs=P(pairs, "y", None),
        check_vma=False,
    )
```

```python
import jax
import jax.numpy as jnp
from jax import lax
from jax.experimental import pallas as pl
from jax.experimental.pallas import tpu as pltpu
from jax.sharding import Mesh
from jax.sharding import PartitionSpec as P

TILES = 8
CAP = 4
NP = TILES * (TILES + 1) // 2
BF = jnp.bfloat16
F32 = jnp.float32
MIB = 1 << 20


def shift(a, axis, d):
    return lax.ppermute(a, axis, [(i, (i + d) % 4) for i in range(4)])


def tie(*arrays):
    return lax.optimization_barrier(arrays)


EARLY_L = [(dc, dz) for dc in range(2) for dz in (0, 1, 3)]
LATE_L = [(dc, 2) for dc in range(2)]


def product(lefts, rights):
    return lax.dot_general(
        jnp.concatenate(lefts, 0),
        jnp.concatenate(rights, 0),
        (((1,), (1,)), ((), ())),
        preferred_element_type=F32,
    )


def store(meta, sums, out, ip, jp, sources, row):
    z, c, y = meta[1], meta[2], meta[3]
    for n, (dc, dz) in enumerate(sources):
        zz, cc = (z + dz) % 4, (c + dc) % 2
        i = 2 * ip + zz // 2
        dy = (2 * (zz % 2) + cc - y + 4) % 4
        for half in range(2):
            j = 2 * jp + (z // 2 + half) % 2
            at = jnp.where(i <= j, j * (j + 1) // 2 + i, NP)
            sums[dy, at] = out[row + 64 * n : row + 64 * n + 64, 128 * half : 128 * half + 128]


def early_kernel(meta, *refs):
    lefts, rights, sums = refs[:6], refs[6:9], refs[9]
    x = meta[0]
    for n, dx in enumerate((0, 1, 3)):
        near_step(meta, lefts, [rights[n]], (x + dx) % 4, sums)


def near_step(meta, lefts, right, jp, sums):
    x = meta[0]

    def step(k, _):
        ip = (x + k) % 4

        @pl.when(ip <= jp)
        def _():
            out = product([ref[k] for ref in lefts], [ref[...] for ref in right])
            store(meta, sums, out, ip, jp, EARLY_L, 0)

        return 0

    lax.fori_loop(0, 4, step, 0)


def middle_kernel(meta, *refs):
    near_step(meta, refs[:6], refs[6:8], (meta[0] + 2) % 4, refs[9])


def late_kernel(meta, *refs):
    late, rights = refs[:4], [refs[4:5], refs[5:6], refs[7:9], refs[6:7]]
    s1, s2, s3, sums = refs[10:14]
    x = meta[0]
    rows = [late[2 * dc + k // 2][k % 2] for k in range(4) for dc in range(2)]
    for dx, right in enumerate(rights):
        jp = (x + dx) % 4
        out = product(rows, [ref[...] for ref in right])
        for k in range(4):
            store(meta, sums, out, (x + k) % 4, jp, LATE_L, 128 * k)
    for k, ref in enumerate((s1, s2, s3)):
        ref[...] = sums[k + 1, :NP].astype(BF)


def grams(kernel, meta, given, sums=None, parts=False):
    width = given[0].shape[-1]
    smem = pl.BlockSpec(memory_space=pltpu.SMEM)
    vmem = pl.BlockSpec(memory_space=pltpu.VMEM)
    shapes = [jax.ShapeDtypeStruct((NP, 64, 128), BF)] * 3 if parts else []
    shapes += [jax.ShapeDtypeStruct((4, NP + 1, 64, 128), F32)]
    aliases = {}
    if sums is not None:
        given = [*given, sums]
        aliases = {len(given): len(shapes) - 1}
    return pl.pallas_call(
        kernel,
        out_shape=shapes,
        in_specs=[smem] + [vmem] * len(given),
        out_specs=[vmem] * len(shapes),
        input_output_aliases=aliases,
        compiler_params=pltpu.CompilerParams(vmem_limit_bytes=16 * MIB),
        cost_estimate=pl.CostEstimate(
            flops=2 * 4 * 512 * 256 * width, bytes_accessed=16 * MIB, transcendentals=0
        ),
        name=kernel.__name__,
    )(meta, *given)


def prepare_kernel(meta, dens, weights, keep, send, *parts):
    k, width = dens.shape[1], keep.shape[1]
    x, z1 = meta[0], meta[1] // 2
    edge = k // 128 * 128
    for ref in (keep, send):
        ref[:, edge:] = jnp.zeros((128, width - edge), BF)
    keep[:, :k] = dens[pl.ds(pl.multiple_of(z1 * 128, 128), 128), :]
    send[:, :k] = dens[pl.ds(pl.multiple_of((1 - z1) * 128, 128), 128), :]
    for d, ref in enumerate(parts):
        ref[0, :, edge:] = jnp.zeros((64, width - edge), BF)
        for h in range(2):
            row = pl.multiple_of(h * 128 + (x + d) % 4 * 32, 32)
            part = dens[pl.ds(row, 32), :].astype(F32) * weights[...]
            ref[0, 32 * h : 32 * h + 32, :k] = part.astype(BF)


def prepare(meta, dens, weights, width):
    smem = pl.BlockSpec(memory_space=pltpu.SMEM)
    vmem = pl.BlockSpec(memory_space=pltpu.VMEM)
    shapes = [jax.ShapeDtypeStruct((128, width), BF)] * 2
    shapes += [jax.ShapeDtypeStruct((1, 64, width), BF)] * 4
    return pl.pallas_call(
        prepare_kernel,
        out_shape=shapes,
        in_specs=[smem, vmem, vmem],
        out_specs=[vmem] * 6,
        compiler_params=pltpu.CompilerParams(vmem_limit_bytes=16 * MIB),
        name="prepare",
    )(meta, dens, weights)


def route_kernel(index, sums, a, b, c, out, total):
    total[:NP] = (
        sums[0, :NP] + a[...].astype(F32) + b[...].astype(F32) + c[...].astype(F32)
    ).astype(BF)
    total[NP] = jnp.zeros(total.shape[1:], BF)

    def some(k, _):
        for n in range(8):
            out[8 * k + n] = total[index[8 * k + n]]
        return 0

    lax.fori_loop(0, out.shape[0] // 8, some, 0)


def route(index, sums, parts):
    smem = pl.BlockSpec(memory_space=pltpu.SMEM)
    vmem = pl.BlockSpec(memory_space=pltpu.VMEM)
    return pl.pallas_call(
        route_kernel,
        out_shape=jax.ShapeDtypeStruct((index.shape[0], 64, 128), BF),
        in_specs=[smem] + [vmem] * 4,
        out_specs=vmem,
        scratch_shapes=[pltpu.VMEM((NP + 1, 64, 128), BF)],
        compiler_params=pltpu.CompilerParams(vmem_limit_bytes=16 * MIB),
        name="route",
    )(index, sums, *parts)


def place_kernel(got, out):
    for src in range(32):
        x, z1, z0, c = src // 8, (src // 4) % 2, (src // 2) % 2, src % 2
        col = (4 * z0 + 2 * c + z1) * 128
        out[0, 32 * x : 32 * x + 32, col : col + 128] = got[src, 0].astype(F32)


def place(got):
    return pl.pallas_call(
        place_kernel,
        grid=(CAP, 2),
        out_shape=jax.ShapeDtypeStruct((CAP, 256, 1024), F32),
        in_specs=[pl.BlockSpec((32, 1, 32, 128), lambda s, h: (0, s, h, 0))],
        out_specs=pl.BlockSpec((1, 128, 1024), lambda s, h: (s, h, 0)),
        name="place",
    )(got)


def on_device(densities, coulomb, pair_list, owner):
    x, z, c, y = (lax.axis_index(n) for n in ("x", "z", "c", "y"))
    k = densities.shape[1]
    meta = jnp.stack([x, z, c, y]).astype(jnp.int32)
    keep, send, *mine = prepare(meta, densities, coulomb[None, :], -(-k // 128) * 128)
    got = shift(send, "z", 2)
    other = [(0, 1), (1, 0)]
    got, e1, e2, e3 = tie(
        got, shift(mine[3], "x", 3), shift(mine[2], "x", 2), shift(mine[1], "x", 1)
    )
    right = jnp.concatenate([keep, got], 0)
    left = jnp.concatenate([mine[0], e1, e2, e3], 0)
    right, left = tie(right, left)

    left3, left1 = shift(left, "z", 1), shift(left, "z", -1)
    right3, right1 = shift(right, "x", 1), shift(right, "x", -1)
    swap0 = lax.ppermute(left, "c", other)
    right3, right1, left3, left1, swap0 = tie(right3, right1, left3, left1, swap0)

    left2a, left2b = shift(left3[:2], "z", 1), shift(left1[2:], "z", -1)
    right2a, right2b = shift(right3[:128], "x", 1), shift(right1[128:], "x", -1)
    swap1, swap3 = lax.ppermute(left1, "c", other), lax.ppermute(left3, "c", other)
    lefts = [left, left1, left3, swap0, swap1, swap3]
    rights = [right, right1, right3]
    (sums,) = grams(early_kernel, meta, lefts + rights)
    left2a, left2b, sums = tie(left2a, left2b, sums)
    swap2a, swap2b = lax.ppermute(left2a, "c", other), lax.ppermute(left2b, "c", other)
    far = [right2a, right2b]
    (sums,) = grams(middle_kernel, meta, lefts + far, sums)
    late = [left2a, left2b, swap2a, swap2b]
    s1, s2, s3, sums = grams(late_kernel, meta, late + rights + far, sums, True)
    parts = [shift(s1, "y", 1), shift(s2, "y", 2), shift(s3, "y", 3)]

    owners = 32
    owner_ids = owner[:, 0]
    onehot = (owner_ids[:, None] == jnp.arange(owners, dtype=jnp.int32)[None, :]).astype(jnp.int32)
    rank = jnp.sum((jnp.cumsum(onehot, 0) - onehot) * onehot, 1)
    slot = owner_ids * CAP + rank
    match = (slot[None, :] == jnp.arange(owners * CAP, dtype=jnp.int32)[:, None]).astype(jnp.int32)
    second = pair_list[:, 1]
    which = second * (second + 1) // 2 + pair_list[:, 0]
    index = NP + jnp.sum(match * (which - NP)[None, :], 1)

    routed = route(index, sums, parts).reshape(owners, CAP, 64, 128)
    arrived = lax.all_to_all(routed, ("x", "z", "c"), 0, 0, tiled=True)
    return place(arrived)


def solution(mesh):
    grid = Mesh(mesh.devices.reshape(4, 4, 2, 4), ("x", "z", "c", "y"))
    pairs = ("x", "z", "c")
    return jax.shard_map(
        on_device,
        mesh=grid,
        in_specs=(P(pairs, "y"), P("y"), P(), P()),
        out_specs=P(pairs, "y", None),
        check_vma=False,
    )
```

```python
import functools

import jax
import jax.numpy as jnp
from jax import lax
from jax.experimental import pallas as pl
from jax.experimental.pallas import tpu as pltpu
from jax.sharding import Mesh
from jax.sharding import PartitionSpec as P

TILES = 8
CAP = 4
NP = TILES * (TILES + 1) // 2
BF = jnp.bfloat16
F32 = jnp.float32
FIRST, SECOND = 18, 20
MIB = 1 << 20


def shift(a, axis, d):
    return lax.ppermute(a, axis, [(i, (i + d) % 4) for i in range(4)])


def tie(*arrays):
    return lax.optimization_barrier(arrays)


EARLY_L = [(dc, dz) for dc in range(2) for dz in (0, 1, 3)]
LATE_L = [(dc, 2) for dc in range(2)]


def product(lefts, rights):
    return lax.dot_general(
        jnp.concatenate(lefts, 0),
        jnp.concatenate(rights, 0),
        (((1,), (1,)), ((), ())),
        preferred_element_type=F32,
    )


def store(meta, sums, out, ip, jp, sources, row):
    z, c, y = meta[1], meta[2], meta[3]
    for n, (dc, dz) in enumerate(sources):
        zz, cc = (z + dz) % 4, (c + dc) % 2
        i = 2 * ip + zz // 2
        dy = (2 * (zz % 2) + cc - y + 4) % 4
        for half in range(2):
            j = 2 * jp + (z // 2 + half) % 2
            at = jnp.where(i <= j, j * (j + 1) // 2 + i, NP)
            sums[dy, at] = out[row + 64 * n : row + 64 * n + 64, 128 * half : 128 * half + 128]


def early_kernel(meta, *refs):
    lefts, rights, sums = refs[:6], refs[6:9], refs[9]
    x = meta[0]
    for n, dx in enumerate((0, 1, 3)):
        near_step(meta, lefts, [rights[n]], (x + dx) % 4, sums)


def near_step(meta, lefts, right, jp, sums):
    x = meta[0]

    def step(k, _):
        ip = (x + k) % 4

        @pl.when(ip <= jp)
        def _():
            out = product([ref[k] for ref in lefts], [ref[...] for ref in right])
            store(meta, sums, out, ip, jp, EARLY_L, 0)

        return 0

    lax.fori_loop(0, 4, step, 0)


def pack(order, sums, outs):
    for p in range(outs[0].shape[0]):
        at = order[p]
        for k, ref in enumerate(outs):
            ref[p] = sums[k + 1, at].astype(BF)


def middle_kernel(meta, order, *refs):
    near_step(meta, refs[:6], refs[6:8], (meta[0] + 2) % 4, refs[12])
    pack(order, refs[12], refs[9:12])


def late_kernel(dc, meta, order, *refs):
    late, rights = refs[:2], [refs[2:3], refs[3:4], refs[5:7], refs[4:5]]
    sums = refs[-1]
    x = meta[0]
    rows = [late[k // 2][k % 2] for k in range(4)]
    for dx, right in enumerate(rights):
        jp = (x + dx) % 4
        out = product(rows, [ref[...] for ref in right])
        for k in range(4):
            store(meta, sums, out, (x + k) % 4, jp, [(dc, 2)], 64 * k)
    if dc:
        pack(order, sums, refs[8:11])


def grams(kernel, name, scalars, given, sums=None, parts=0):
    width = given[0].shape[-1]
    smem = pl.BlockSpec(memory_space=pltpu.SMEM)
    vmem = pl.BlockSpec(memory_space=pltpu.VMEM)
    shapes = [jax.ShapeDtypeStruct((parts, 64, 128), BF)] * 3 if parts else []
    shapes += [jax.ShapeDtypeStruct((4, NP + 1, 64, 128), F32)]
    aliases = {}
    if sums is not None:
        given = [*given, sums]
        aliases = {len(scalars) + len(given) - 1: len(shapes) - 1}
    return pl.pallas_call(
        kernel,
        out_shape=shapes,
        in_specs=[smem] * len(scalars) + [vmem] * len(given),
        out_specs=[vmem] * len(shapes),
        input_output_aliases=aliases,
        compiler_params=pltpu.CompilerParams(vmem_limit_bytes=16 * MIB),
        cost_estimate=pl.CostEstimate(
            flops=2 * 4 * 512 * 256 * width, bytes_accessed=MIB, transcendentals=0
        ),
        name=name,
    )(*scalars, *given)


def prepare_kernel(meta, dens, weights, keep, send, *parts):
    k, width = dens.shape[1], keep.shape[1]
    x, z1 = meta[0], meta[1] // 2
    edge = k // 128 * 128
    for ref in (keep, send):
        ref[:, edge:] = jnp.zeros((128, width - edge), BF)
    keep[:, :k] = dens[pl.ds(pl.multiple_of(z1 * 128, 128), 128), :]
    send[:, :k] = dens[pl.ds(pl.multiple_of((1 - z1) * 128, 128), 128), :]
    for d, ref in enumerate(parts):
        ref[0, :, edge:] = jnp.zeros((64, width - edge), BF)
        for h in range(2):
            row = pl.multiple_of(h * 128 + (x + d) % 4 * 32, 32)
            part = dens[pl.ds(row, 32), :].astype(F32) * weights[...]
            ref[0, 32 * h : 32 * h + 32, :k] = part.astype(BF)


def prepare(meta, dens, weights, width):
    smem = pl.BlockSpec(memory_space=pltpu.SMEM)
    vmem = pl.BlockSpec(memory_space=pltpu.VMEM)
    shapes = [jax.ShapeDtypeStruct((128, width), BF)] * 2
    shapes += [jax.ShapeDtypeStruct((1, 64, width), BF)] * 4
    return pl.pallas_call(
        prepare_kernel,
        out_shape=shapes,
        in_specs=[smem, vmem, vmem],
        out_specs=[vmem] * 6,
        compiler_params=pltpu.CompilerParams(vmem_limit_bytes=16 * MIB),
        name="prepare",
    )(meta, dens, weights)


def route_kernel(index, order1, order2, sums, *refs):
    out, total = refs[6], refs[7]
    for order, parts in ((order1, refs[:3]), (order2, refs[3:6])):
        for p in range(parts[0].shape[0]):
            at = order[p]
            value = sums[0, at]
            for part in parts:
                value = value + part[p].astype(F32)
            total[at] = value.astype(BF)
    total[NP] = jnp.zeros(total.shape[1:], BF)

    def some(k, _):
        for n in range(8):
            out[8 * k + n] = total[index[8 * k + n]]
        return 0

    lax.fori_loop(0, out.shape[0] // 8, some, 0)


def route(scalars, sums, parts):
    smem = pl.BlockSpec(memory_space=pltpu.SMEM)
    vmem = pl.BlockSpec(memory_space=pltpu.VMEM)
    return pl.pallas_call(
        route_kernel,
        out_shape=jax.ShapeDtypeStruct((scalars[0].shape[0], 64, 128), BF),
        in_specs=[smem] * 3 + [vmem] * 7,
        out_specs=vmem,
        scratch_shapes=[pltpu.VMEM((NP + 1, 64, 128), BF)],
        compiler_params=pltpu.CompilerParams(vmem_limit_bytes=16 * MIB),
        name="route",
    )(*scalars, sums, *parts)


def plan_kernel(meta, first, second, owner, index, order1, order2, count):
    def clear(k, _):
        index[k] = NP
        return 0

    def reset(k, _):
        count[k] = 0
        order1[lax.rem(k, FIRST + 1)] = NP
        order2[lax.rem(k, SECOND + 1)] = NP
        return 0

    def entry(e, _):
        who = owner[e]
        rank = count[who]
        count[who] = rank + 1
        j = second[e]
        index[who * CAP + rank] = j * (j + 1) // 2 + first[e]
        return 0

    lax.fori_loop(0, index.shape[0], clear, 0)
    lax.fori_loop(0, count.shape[0], reset, 0)
    lax.fori_loop(0, owner.shape[0], entry, 0)
    z1 = meta[1] // 2
    n1 = n2 = jnp.int32(0)
    for j in range(TILES):
        for i in range(j + 1):
            one = jnp.where((z1 == i % 2) & (n1 < FIRST), 1, 0)
            order1[jnp.where(one == 1, n1, FIRST)] = j * (j + 1) // 2 + i
            order2[jnp.where(one == 1, SECOND, n2)] = j * (j + 1) // 2 + i
            n1, n2 = n1 + one, n2 + 1 - one


def plan(meta, pair_list, owner, slots):
    smem = pl.BlockSpec(memory_space=pltpu.SMEM)
    return pl.pallas_call(
        plan_kernel,
        out_shape=[jax.ShapeDtypeStruct((n,), jnp.int32) for n in (slots, FIRST + 1, SECOND + 1)],
        in_specs=[smem] * 4,
        out_specs=[smem] * 3,
        scratch_shapes=[pltpu.SMEM((slots // CAP,), jnp.int32)],
        compiler_params=pltpu.CompilerParams(vmem_limit_bytes=MIB),
        name="plan",
    )(meta, pair_list[:, 0], pair_list[:, 1], owner[:, 0])


def place_kernel(got, out):
    for src in range(32):
        x, z1, z0, c = src // 8, (src // 4) % 2, (src // 2) % 2, src % 2
        col = (4 * z0 + 2 * c + z1) * 128
        for h in range(2):
            row = h * 128 + x * 32
            out[0, row : row + 32, col : col + 128] = got[src, 0, 32 * h : 32 * h + 32].astype(F32)


def place(got):
    return pl.pallas_call(
        place_kernel,
        grid=(CAP,),
        out_shape=jax.ShapeDtypeStruct((CAP, 256, 1024), F32),
        in_specs=[pl.BlockSpec((32, 1, 64, 128), lambda s: (0, s, 0, 0))],
        out_specs=pl.BlockSpec((1, 256, 1024), lambda s: (s, 0, 0)),
        name="place",
    )(got)


def on_device(densities, coulomb, pair_list, owner):
    x, z, c, y = (lax.axis_index(n) for n in ("x", "z", "c", "y"))
    k = densities.shape[1]
    meta = jnp.stack([x, z, c, y]).astype(jnp.int32)
    keep, send, *mine = prepare(meta, densities, coulomb[None, :], -(-k // 128) * 128)
    got = shift(send, "z", 2)
    other = [(0, 1), (1, 0)]
    got, e1, e2, e3 = tie(
        got, shift(mine[3], "x", 3), shift(mine[2], "x", 2), shift(mine[1], "x", 1)
    )
    right = jnp.concatenate([keep, got], 0)
    left = jnp.concatenate([mine[0], e1, e2, e3], 0)
    right, left = tie(right, left)

    left3, left1 = shift(left, "z", 1), shift(left, "z", -1)
    right3, right1 = shift(right, "x", 1), shift(right, "x", -1)
    swap0 = lax.ppermute(left, "c", other)
    right3, right1, left3, left1, swap0 = tie(right3, right1, left3, left1, swap0)

    left2a, left2b = shift(left3[:2], "z", 1), shift(left1[2:], "z", -1)
    right2a, right2b = shift(right3[:128], "x", 1), shift(right1[128:], "x", -1)
    index, order1, order2 = plan(meta, pair_list, owner, 32 * CAP)
    index, near1, near3 = tie(index, left1, left3)
    swap1, swap3 = lax.ppermute(near1, "c", other), lax.ppermute(near3, "c", other)
    lefts = [left, left1, left3, swap0, swap1, swap3]
    rights = [right, right1, right3]
    (sums,) = grams(early_kernel, "early", [meta], lefts + rights)
    left2a, left2b, sums = tie(left2a, left2b, sums)
    swap2a, swap2b = lax.ppermute(left2a, "c", other), lax.ppermute(left2b, "c", other)
    far = [right2a, right2b]

    def over_y(blocks):
        return [shift(block, "y", k + 1) for k, block in enumerate(blocks)]

    *blocks, sums = grams(middle_kernel, "middle", [meta, order1], lefts + far, sums, FIRST)
    parts = over_y(blocks)
    late = functools.partial(late_kernel, 0)
    (sums,) = grams(late, "late_own", [meta, order2], [left2a, left2b] + rights + far, sums)
    late = functools.partial(late_kernel, 1)
    *blocks, sums = grams(
        late, "late_other", [meta, order2], [swap2a, swap2b] + rights + far, sums, SECOND
    )
    blocks[1], parts[0], parts[2] = tie(blocks[1], parts[0], parts[2])
    parts += over_y(blocks)

    routed = route([index, order1, order2], sums, parts).reshape(32, CAP, 64, 128)
    arrived = lax.all_to_all(routed, ("x", "z", "c"), 0, 0, tiled=True)
    return place(arrived)


def solution(mesh):
    grid = Mesh(mesh.devices.reshape(4, 4, 2, 4), ("x", "z", "c", "y"))
    pairs = ("x", "z", "c")
    return jax.shard_map(
        on_device,
        mesh=grid,
        in_specs=(P(pairs, "y"), P("y"), P(), P()),
        out_specs=P(pairs, "y", None),
        check_vma=False,
    )
```

```python
import functools

import jax
import jax.numpy as jnp
from jax import lax
from jax.experimental import pallas as pl
from jax.experimental.pallas import tpu as pltpu
from jax.sharding import Mesh
from jax.sharding import PartitionSpec as P

TILES = 8
CAP = 4
NP = TILES * (TILES + 1) // 2
BF = jnp.bfloat16
F32 = jnp.float32
FIRST, SECOND = 18, 20
NEAR = 9
MIB = 1 << 20


def shift(a, axis, d):
    return lax.ppermute(a, axis, [(i, (i + d) % 4) for i in range(4)])


def tie(*arrays):
    return lax.optimization_barrier(arrays)


EARLY_L = [(dc, dz) for dc in range(2) for dz in (0, 1, 3)]
LATE_L = [(dc, 2) for dc in range(2)]


def product(lefts, rights):
    return lax.dot_general(
        jnp.concatenate(lefts, 0),
        jnp.concatenate(rights, 0),
        (((1,), (1,)), ((), ())),
        preferred_element_type=F32,
    )


def store(meta, sums, out, ip, jp, sources, row):
    z, c, y = meta[1], meta[2], meta[3]
    for n, (dc, dz) in enumerate(sources):
        zz, cc = (z + dz) % 4, (c + dc) % 2
        i = 2 * ip + zz // 2
        dy = (2 * (zz % 2) + cc - y + 4) % 4
        for half in range(2):
            j = 2 * jp + (z // 2 + half) % 2
            at = jnp.where(i <= j, j * (j + 1) // 2 + i, NP)
            sums[dy, at] = out[row + 64 * n : row + 64 * n + 64, 128 * half : 128 * half + 128]


def early_kernel(meta, order, *refs):
    lefts, rights, sums = refs[:6], refs[6:9], refs[10]
    x = meta[0]
    for n, dx in enumerate((0, 1, 3)):
        near_step(meta, lefts, [rights[n]], (x + dx) % 4, sums)
    pack(order, sums, {2: refs[9]})


def near_step(meta, lefts, right, jp, sums):
    x = meta[0]

    def step(k, _):
        ip = (x + k) % 4

        @pl.when(ip <= jp)
        def _():
            out = product([ref[k] for ref in lefts], [ref[...] for ref in right])
            store(meta, sums, out, ip, jp, EARLY_L, 0)

        return 0

    lax.fori_loop(0, 4, step, 0)


def pack(order, sums, outs, first=0):
    for k, ref in outs.items():
        for p in range(ref.shape[0]):
            ref[p] = sums[k, order[first + p]].astype(BF)


def middle_kernel(meta, order, *refs):
    near_step(meta, refs[:6], refs[6:8], (meta[0] + 2) % 4, refs[12])
    pack(order, refs[12], {1: refs[9], 3: refs[11]})
    pack(order, refs[12], {2: refs[10]}, NEAR)


def late_kernel(dc, meta, order, *refs):
    late, rights = refs[:2], [refs[2:3], refs[3:4], refs[5:7], refs[4:5]]
    sums = refs[-1]
    x = meta[0]
    rows = [late[k // 2][k % 2] for k in range(4)]
    for dx, right in enumerate(rights):
        jp = (x + dx) % 4
        out = product(rows, [ref[...] for ref in right])
        for k in range(4):
            store(meta, sums, out, (x + k) % 4, jp, [(dc, 2)], 64 * k)
    if dc:
        pack(order, sums, dict(zip((1, 2, 3), refs[8:11])))


def grams(kernel, name, scalars, given, sums=None, parts=()):
    width = given[0].shape[-1]
    smem = pl.BlockSpec(memory_space=pltpu.SMEM)
    vmem = pl.BlockSpec(memory_space=pltpu.VMEM)
    shapes = [jax.ShapeDtypeStruct((n, 64, 128), BF) for n in parts]
    shapes += [jax.ShapeDtypeStruct((4, NP + 1, 64, 128), F32)]
    aliases = {}
    if sums is not None:
        given = [*given, sums]
        aliases = {len(scalars) + len(given) - 1: len(shapes) - 1}
    return pl.pallas_call(
        kernel,
        out_shape=shapes,
        in_specs=[smem] * len(scalars) + [vmem] * len(given),
        out_specs=[vmem] * len(shapes),
        input_output_aliases=aliases,
        compiler_params=pltpu.CompilerParams(vmem_limit_bytes=16 * MIB),
        cost_estimate=pl.CostEstimate(
            flops=2 * 4 * 512 * 256 * width, bytes_accessed=MIB, transcendentals=0
        ),
        name=name,
    )(*scalars, *given)


def prepare_kernel(meta, dens, weights, keep, send, *parts):
    k, width = dens.shape[1], keep.shape[1]
    x, z1 = meta[0], meta[1] // 2
    edge = k // 128 * 128
    for ref in (keep, send):
        ref[:, edge:] = jnp.zeros((128, width - edge), BF)
    keep[:, :k] = dens[pl.ds(pl.multiple_of(z1 * 128, 128), 128), :]
    send[:, :k] = dens[pl.ds(pl.multiple_of((1 - z1) * 128, 128), 128), :]
    for d, ref in enumerate(parts):
        ref[0, :, edge:] = jnp.zeros((64, width - edge), BF)
        for h in range(2):
            row = pl.multiple_of(h * 128 + (x + d) % 4 * 32, 32)
            part = dens[pl.ds(row, 32), :].astype(F32) * weights[...]
            ref[0, 32 * h : 32 * h + 32, :k] = part.astype(BF)


def prepare(meta, dens, weights, width):
    smem = pl.BlockSpec(memory_space=pltpu.SMEM)
    vmem = pl.BlockSpec(memory_space=pltpu.VMEM)
    shapes = [jax.ShapeDtypeStruct((128, width), BF)] * 2
    shapes += [jax.ShapeDtypeStruct((1, 64, width), BF)] * 4
    return pl.pallas_call(
        prepare_kernel,
        out_shape=shapes,
        in_specs=[smem, vmem, vmem],
        out_specs=[vmem] * 6,
        compiler_params=pltpu.CompilerParams(vmem_limit_bytes=16 * MIB),
        name="prepare",
    )(meta, dens, weights)


def route_kernel(index, order1, order2, sums, *refs):
    near2, one1, one2, one3, two1, two2, two3, out, total = refs
    for p in range(FIRST):
        at = order1[p]
        opposite = near2[p] if p < NEAR else one2[p - NEAR]
        value = sums[0, at] + one1[p].astype(F32) + opposite.astype(F32)
        total[at] = (value + one3[p].astype(F32)).astype(BF)
    for p in range(SECOND):
        at = order2[p]
        value = sums[0, at] + two1[p].astype(F32) + two2[p].astype(F32)
        total[at] = (value + two3[p].astype(F32)).astype(BF)
    total[NP] = jnp.zeros(total.shape[1:], BF)

    def some(k, _):
        for n in range(8):
            out[8 * k + n] = total[index[8 * k + n]]
        return 0

    lax.fori_loop(0, out.shape[0] // 8, some, 0)


def route(scalars, sums, parts):
    smem = pl.BlockSpec(memory_space=pltpu.SMEM)
    vmem = pl.BlockSpec(memory_space=pltpu.VMEM)
    return pl.pallas_call(
        route_kernel,
        out_shape=jax.ShapeDtypeStruct((scalars[0].shape[0], 64, 128), BF),
        in_specs=[smem] * 3 + [vmem] * 8,
        out_specs=vmem,
        scratch_shapes=[pltpu.VMEM((NP + 1, 64, 128), BF)],
        compiler_params=pltpu.CompilerParams(vmem_limit_bytes=16 * MIB),
        name="route",
    )(*scalars, sums, *parts)


def plan_kernel(meta, first, second, owner, index, order1, order2, count):
    def clear(k, _):
        index[k] = NP
        return 0

    def reset(k, _):
        count[k] = 0
        order1[lax.rem(k, FIRST + 1)] = NP
        order2[lax.rem(k, SECOND + 1)] = NP
        return 0

    def entry(e, _):
        who = owner[e]
        rank = count[who]
        count[who] = rank + 1
        j = second[e]
        index[who * CAP + rank] = j * (j + 1) // 2 + first[e]
        return 0

    lax.fori_loop(0, index.shape[0], clear, 0)
    lax.fori_loop(0, count.shape[0], reset, 0)
    lax.fori_loop(0, owner.shape[0], entry, 0)
    far, z1 = (meta[0] + 2) % 4, meta[1] // 2
    n0, n1, n2 = jnp.int32(0), jnp.int32(NEAR), jnp.int32(0)
    for j in range(TILES):
        for i in range(j + 1):
            mine = z1 == i % 2
            zero = jnp.where(mine & (far != j // 2) & (n0 < NEAR), 1, 0)
            one = jnp.where(mine & (zero == 0) & (n1 < FIRST), 1, 0)
            at = jnp.where(zero == 1, n0, jnp.where(one == 1, n1, FIRST))
            order1[at] = j * (j + 1) // 2 + i
            order2[jnp.where(zero + one == 1, SECOND, n2)] = j * (j + 1) // 2 + i
            n0, n1, n2 = n0 + zero, n1 + one, n2 + 1 - zero - one


def plan(meta, pair_list, owner, slots):
    smem = pl.BlockSpec(memory_space=pltpu.SMEM)
    return pl.pallas_call(
        plan_kernel,
        out_shape=[jax.ShapeDtypeStruct((n,), jnp.int32) for n in (slots, FIRST + 1, SECOND + 1)],
        in_specs=[smem] * 4,
        out_specs=[smem] * 3,
        scratch_shapes=[pltpu.SMEM((slots // CAP,), jnp.int32)],
        compiler_params=pltpu.CompilerParams(vmem_limit_bytes=MIB),
        name="plan",
    )(meta, pair_list[:, 0], pair_list[:, 1], owner[:, 0])


def place_kernel(got, out):
    for src in range(32):
        x, z1, z0, c = src // 8, (src // 4) % 2, (src // 2) % 2, src % 2
        col = (4 * z0 + 2 * c + z1) * 128
        for h in range(2):
            row = h * 128 + x * 32
            out[0, row : row + 32, col : col + 128] = got[src, 0, 32 * h : 32 * h + 32].astype(F32)


def place(got):
    return pl.pallas_call(
        place_kernel,
        grid=(CAP,),
        out_shape=jax.ShapeDtypeStruct((CAP, 256, 1024), F32),
        in_specs=[pl.BlockSpec((32, 1, 64, 128), lambda s: (0, s, 0, 0))],
        out_specs=pl.BlockSpec((1, 256, 1024), lambda s: (s, 0, 0)),
        name="place",
    )(got)


def on_device(densities, coulomb, pair_list, owner):
    x, z, c, y = (lax.axis_index(n) for n in ("x", "z", "c", "y"))
    k = densities.shape[1]
    meta = jnp.stack([x, z, c, y]).astype(jnp.int32)
    keep, send, *mine = prepare(meta, densities, coulomb[None, :], -(-k // 128) * 128)
    got = shift(send, "z", 2)
    other = [(0, 1), (1, 0)]
    got, e1, e2, e3 = tie(
        got, shift(mine[3], "x", 3), shift(mine[2], "x", 2), shift(mine[1], "x", 1)
    )
    right = jnp.concatenate([keep, got], 0)
    left = jnp.concatenate([mine[0], e1, e2, e3], 0)
    right, left = tie(right, left)

    left3, left1 = shift(left, "z", 1), shift(left, "z", -1)
    right3, right1 = shift(right, "x", 1), shift(right, "x", -1)
    swap0 = lax.ppermute(left, "c", other)
    right3, right1 = tie(right3, right1)

    right2a, right2b = shift(right3[:128], "x", 1), shift(right1[128:], "x", -1)
    left2a, left2b = shift(left3[:2], "z", 1), shift(left1[2:], "z", -1)
    index, order1, order2 = plan(meta, pair_list, owner, 32 * CAP)
    index, near1, near3 = tie(index, left1, left3)
    swap1, swap3 = lax.ppermute(near1, "c", other), lax.ppermute(near3, "c", other)
    lefts = [left, left1, left3, swap0, swap1, swap3]
    rights = [right, right1, right3]
    near2, sums = grams(early_kernel, "early", [meta, order1], lefts + rights, parts=[NEAR])
    near2 = shift(near2, "y", 2)
    left2a, left2b, sums, near2 = tie(left2a, left2b, sums, near2)
    swap2a, swap2b = lax.ppermute(left2a, "c", other), lax.ppermute(left2b, "c", other)
    far = [right2a, right2b]

    def over_y(blocks):
        return [shift(block, "y", k + 1) for k, block in enumerate(blocks)]

    *blocks, sums = grams(
        middle_kernel, "middle", [meta, order1], lefts + far, sums, [FIRST, FIRST - NEAR, FIRST]
    )
    parts = over_y(blocks)
    late = functools.partial(late_kernel, 0)
    (sums,) = grams(late, "late_own", [meta, order2], [left2a, left2b] + rights + far, sums)
    late = functools.partial(late_kernel, 1)
    *blocks, sums = grams(
        late, "late_other", [meta, order2], [swap2a, swap2b] + rights + far, sums, [SECOND] * 3
    )
    blocks[1], parts[0], parts[2] = tie(blocks[1], parts[0], parts[2])
    parts += over_y(blocks)

    routed = route([index, order1, order2], sums, [near2] + parts).reshape(32, CAP, 64, 128)
    arrived = lax.all_to_all(routed, ("x", "z", "c"), 0, 0, tiled=True)
    return place(arrived)


def solution(mesh):
    grid = Mesh(mesh.devices.reshape(4, 4, 2, 4), ("x", "z", "c", "y"))
    pairs = ("x", "z", "c")
    return jax.shard_map(
        on_device,
        mesh=grid,
        in_specs=(P(pairs, "y"), P("y"), P(), P()),
        out_specs=P(pairs, "y", None),
        check_vma=False,
    )
```

```python
import functools

import jax
import jax.numpy as jnp
from jax import lax
from jax.experimental import pallas as pl
from jax.experimental.pallas import tpu as pltpu
from jax.sharding import Mesh
from jax.sharding import PartitionSpec as P

TILES = 8
CAP = 4
NP = TILES * (TILES + 1) // 2
BF = jnp.bfloat16
F32 = jnp.float32
FIRST, SECOND = 16, 20
NEAR = 9
MIB = 1 << 20


def shift(a, axis, d):
    return lax.ppermute(a, axis, [(i, (i + d) % 4) for i in range(4)])


def tie(*arrays):
    return lax.optimization_barrier(arrays)


EARLY_L = [(dc, dz) for dc in range(2) for dz in (0, 1, 3)]
LATE_L = [(dc, 2) for dc in range(2)]


def product(lefts, rights):
    return lax.dot_general(
        jnp.concatenate(lefts, 0),
        jnp.concatenate(rights, 0),
        (((1,), (1,)), ((), ())),
        preferred_element_type=F32,
    )


def store(meta, sums, out, ip, jp, sources, row):
    z, c, y = meta[1], meta[2], meta[3]
    for n, (dc, dz) in enumerate(sources):
        zz, cc = (z + dz) % 4, (c + dc) % 2
        i = 2 * ip + zz // 2
        dy = (2 * (zz % 2) + cc - y + 4) % 4
        for half in range(2):
            j = 2 * jp + (z // 2 + half) % 2
            at = jnp.where(i <= j, j * (j + 1) // 2 + i, NP)
            sums[dy, at] = out[row + 64 * n : row + 64 * n + 64, 128 * half : 128 * half + 128]


def early_kernel(meta, order, *refs):
    lefts, rights, sums = refs[:6], refs[6:9], refs[10]
    x = meta[0]
    for n, dx in enumerate((0, 1, 3)):
        near_step(meta, lefts, [rights[n]], (x + dx) % 4, sums)
    pack(sums, 2, order, 0, NEAR, refs[9])


def near_step(meta, lefts, right, jp, sums):
    x = meta[0]

    def step(k, _):
        ip = (x + k) % 4

        @pl.when(ip <= jp)
        def _():
            out = product([ref[k] for ref in lefts], [ref[...] for ref in right])
            store(meta, sums, out, ip, jp, EARLY_L, 0)

        return 0

    lax.fori_loop(0, 4, step, 0)


def pack(sums, dy, order, first, size, ref, at=0):
    for p in range(size):
        ref[at + p] = sums[dy, order[first + p]].astype(BF)


def middle_kernel(meta, order, *refs):
    near_step(meta, refs[:6], refs[6:8], (meta[0] + 2) % 4, refs[11])
    pack(refs[11], 1, order, 0, FIRST, refs[9])
    pack(refs[11], 3, order, 0, FIRST, refs[10])


def late_kernel(dc, meta, order1, order2, *refs):
    late, rights = refs[:2], [refs[2:3], refs[3:4], refs[5:7], refs[4:5]]
    sums = refs[-1]
    x = meta[0]
    rows = [late[k // 2][k % 2] for k in range(4)]
    for dx, right in enumerate(rights):
        jp = (x + dx) % 4
        out = product(rows, [ref[...] for ref in right])
        for k in range(4):
            store(meta, sums, out, (x + k) % 4, jp, [(dc, 2)], 64 * k)
    if dc:
        pack(sums, 1, order2, 0, SECOND, refs[8])
        pack(sums, 2, order1, NEAR, FIRST - NEAR, refs[9])
        pack(sums, 2, order2, 0, SECOND, refs[9], FIRST - NEAR)
        pack(sums, 3, order2, 0, SECOND, refs[10])


def grams(kernel, name, scalars, given, sums=None, parts=()):
    width = given[0].shape[-1]
    smem = pl.BlockSpec(memory_space=pltpu.SMEM)
    vmem = pl.BlockSpec(memory_space=pltpu.VMEM)
    shapes = [jax.ShapeDtypeStruct((n, 64, 128), BF) for n in parts]
    shapes += [jax.ShapeDtypeStruct((4, NP + 1, 64, 128), F32)]
    aliases = {}
    if sums is not None:
        given = [*given, sums]
        aliases = {len(scalars) + len(given) - 1: len(shapes) - 1}
    return pl.pallas_call(
        kernel,
        out_shape=shapes,
        in_specs=[smem] * len(scalars) + [vmem] * len(given),
        out_specs=[vmem] * len(shapes),
        input_output_aliases=aliases,
        compiler_params=pltpu.CompilerParams(vmem_limit_bytes=16 * MIB),
        cost_estimate=pl.CostEstimate(
            flops=2 * 4 * 512 * 256 * width, bytes_accessed=MIB, transcendentals=0
        ),
        name=name,
    )(*scalars, *given)


def prepare_kernel(meta, dens, weights, keep, send, *parts):
    k, width = dens.shape[1], keep.shape[1]
    x, z1 = meta[0], meta[1] // 2
    edge = k // 128 * 128
    for ref in (keep, send):
        ref[:, edge:] = jnp.zeros((128, width - edge), BF)
    keep[:, :k] = dens[pl.ds(pl.multiple_of(z1 * 128, 128), 128), :]
    send[:, :k] = dens[pl.ds(pl.multiple_of((1 - z1) * 128, 128), 128), :]
    for d, ref in enumerate(parts):
        ref[0, :, edge:] = jnp.zeros((64, width - edge), BF)
        for h in range(2):
            row = pl.multiple_of(h * 128 + (x + d) % 4 * 32, 32)
            part = dens[pl.ds(row, 32), :].astype(F32) * weights[...]
            ref[0, 32 * h : 32 * h + 32, :k] = part.astype(BF)


def prepare(meta, dens, weights, width):
    smem = pl.BlockSpec(memory_space=pltpu.SMEM)
    vmem = pl.BlockSpec(memory_space=pltpu.VMEM)
    shapes = [jax.ShapeDtypeStruct((128, width), BF)] * 2
    shapes += [jax.ShapeDtypeStruct((1, 64, width), BF)] * 4
    return pl.pallas_call(
        prepare_kernel,
        out_shape=shapes,
        in_specs=[smem, vmem, vmem],
        out_specs=[vmem] * 6,
        compiler_params=pltpu.CompilerParams(vmem_limit_bytes=16 * MIB),
        name="prepare",
    )(meta, dens, weights)


def route_kernel(index, order1, order2, sums, *refs):
    near2, one1, one3, two1, two2, two3, out, total = refs
    for p in range(FIRST):
        at = order1[p]
        opposite = near2[p] if p < NEAR else two2[p - NEAR]
        value = sums[0, at] + one1[p].astype(F32) + opposite.astype(F32)
        total[at] = (value + one3[p].astype(F32)).astype(BF)
    for p in range(SECOND):
        at = order2[p]
        value = sums[0, at] + two1[p].astype(F32) + two2[FIRST - NEAR + p].astype(F32)
        total[at] = (value + two3[p].astype(F32)).astype(BF)
    total[NP] = jnp.zeros(total.shape[1:], BF)

    def some(k, _):
        for n in range(8):
            out[8 * k + n] = total[index[8 * k + n]]
        return 0

    lax.fori_loop(0, out.shape[0] // 8, some, 0)


def route(scalars, sums, parts):
    smem = pl.BlockSpec(memory_space=pltpu.SMEM)
    vmem = pl.BlockSpec(memory_space=pltpu.VMEM)
    return pl.pallas_call(
        route_kernel,
        out_shape=jax.ShapeDtypeStruct((scalars[0].shape[0], 64, 128), BF),
        in_specs=[smem] * 3 + [vmem] * 7,
        out_specs=vmem,
        scratch_shapes=[pltpu.VMEM((NP + 1, 64, 128), BF)],
        compiler_params=pltpu.CompilerParams(vmem_limit_bytes=16 * MIB),
        name="route",
    )(*scalars, sums, *parts)


def plan_kernel(meta, first, second, owner, index, order1, order2, count):
    def clear(k, _):
        index[k] = NP
        return 0

    def reset(k, _):
        count[k] = 0
        order1[lax.rem(k, FIRST + 1)] = NP
        order2[lax.rem(k, SECOND + 1)] = NP
        return 0

    def entry(e, _):
        who = owner[e]
        rank = count[who]
        count[who] = rank + 1
        j = second[e]
        index[who * CAP + rank] = j * (j + 1) // 2 + first[e]
        return 0

    lax.fori_loop(0, index.shape[0], clear, 0)
    lax.fori_loop(0, count.shape[0], reset, 0)
    lax.fori_loop(0, owner.shape[0], entry, 0)
    far, z1 = (meta[0] + 2) % 4, meta[1] // 2
    n0, n1, n2 = jnp.int32(0), jnp.int32(NEAR), jnp.int32(0)
    for j in range(TILES):
        for i in range(j + 1):
            mine = z1 == i % 2
            zero = jnp.where(mine & (far != j // 2) & (n0 < NEAR), 1, 0)
            one = jnp.where(mine & (zero == 0) & (n1 < FIRST), 1, 0)
            at = jnp.where(zero == 1, n0, jnp.where(one == 1, n1, FIRST))
            order1[at] = j * (j + 1) // 2 + i
            order2[jnp.where(zero + one == 1, SECOND, n2)] = j * (j + 1) // 2 + i
            n0, n1, n2 = n0 + zero, n1 + one, n2 + 1 - zero - one


def plan(meta, pair_list, owner, slots):
    smem = pl.BlockSpec(memory_space=pltpu.SMEM)
    return pl.pallas_call(
        plan_kernel,
        out_shape=[jax.ShapeDtypeStruct((n,), jnp.int32) for n in (slots, FIRST + 1, SECOND + 1)],
        in_specs=[smem] * 4,
        out_specs=[smem] * 3,
        scratch_shapes=[pltpu.SMEM((slots // CAP,), jnp.int32)],
        compiler_params=pltpu.CompilerParams(vmem_limit_bytes=MIB),
        name="plan",
    )(meta, pair_list[:, 0], pair_list[:, 1], owner[:, 0])


def place_kernel(got, out):
    for src in range(32):
        x, z1, z0, c = src // 8, (src // 4) % 2, (src // 2) % 2, src % 2
        col = (4 * z0 + 2 * c + z1) * 128
        for h in range(2):
            row = h * 128 + x * 32
            out[0, row : row + 32, col : col + 128] = got[src, 0, 32 * h : 32 * h + 32].astype(F32)


def place(got):
    return pl.pallas_call(
        place_kernel,
        grid=(CAP,),
        out_shape=jax.ShapeDtypeStruct((CAP, 256, 1024), F32),
        in_specs=[pl.BlockSpec((32, 1, 64, 128), lambda s: (0, s, 0, 0))],
        out_specs=pl.BlockSpec((1, 256, 1024), lambda s: (s, 0, 0)),
        name="place",
    )(got)


def on_device(densities, coulomb, pair_list, owner):
    x, z, c, y = (lax.axis_index(n) for n in ("x", "z", "c", "y"))
    k = densities.shape[1]
    meta = jnp.stack([x, z, c, y]).astype(jnp.int32)
    keep, send, *mine = prepare(meta, densities, coulomb[None, :], -(-k // 128) * 128)
    got = shift(send, "z", 2)
    other = [(0, 1), (1, 0)]
    got, e1, e2, e3 = tie(
        got, shift(mine[3], "x", 3), shift(mine[2], "x", 2), shift(mine[1], "x", 1)
    )
    right = jnp.concatenate([keep, got], 0)
    left = jnp.concatenate([mine[0], e1, e2, e3], 0)
    right, left = tie(right, left)

    left3, left1 = shift(left, "z", 1), shift(left, "z", -1)
    right3, right1 = shift(right, "x", 1), shift(right, "x", -1)
    swap0 = lax.ppermute(left, "c", other)
    right3, right1 = tie(right3, right1)

    right2a, right2b = shift(right3[:128], "x", 1), shift(right1[128:], "x", -1)
    left2a, left2b = shift(left3[:2], "z", 1), shift(left1[2:], "z", -1)
    index, order1, order2 = plan(meta, pair_list, owner, 32 * CAP)
    index, near1, near3 = tie(index, left1, left3)
    swap1, swap3 = lax.ppermute(near1, "c", other), lax.ppermute(near3, "c", other)
    lefts = [left, left1, left3, swap0, swap1, swap3]
    rights = [right, right1, right3]
    near2, sums = grams(early_kernel, "early", [meta, order1], lefts + rights, parts=[NEAR])
    near2 = shift(near2, "y", 2)
    left2a, left2b, sums, near2 = tie(left2a, left2b, sums, near2)
    swap2a, swap2b = lax.ppermute(left2a, "c", other), lax.ppermute(left2b, "c", other)
    far = [right2a, right2b]

    one1, one3, sums = grams(middle_kernel, "middle", [meta, order1], lefts + far, sums, [FIRST] * 2)
    one1, one3 = shift(one1, "y", 1), shift(one3, "y", 3)
    scalars = [meta, order1, order2]
    late = functools.partial(late_kernel, 0)
    (sums,) = grams(late, "late_own", scalars, [left2a, left2b] + rights + far, sums)
    late = functools.partial(late_kernel, 1)
    sizes = [SECOND, FIRST - NEAR + SECOND, SECOND]
    *two, sums = grams(
        late, "late_other", scalars, [swap2a, swap2b] + rights + far, sums, sizes
    )
    two[0], two[2], one1, one3 = tie(two[0], two[2], one1, one3)
    two = [shift(block, "y", k + 1) for k, block in enumerate(two)]

    routed = route([index, order1, order2], sums, [near2, one1, one3, *two]).reshape(32, CAP, 64, 128)
    arrived = lax.all_to_all(routed, ("x", "z", "c"), 0, 0, tiled=True)
    return place(arrived)


def solution(mesh):
    grid = Mesh(mesh.devices.reshape(4, 4, 2, 4), ("x", "z", "c", "y"))
    pairs = ("x", "z", "c")
    return jax.shard_map(
        on_device,
        mesh=grid,
        in_specs=(P(pairs, "y"), P("y"), P(), P()),
        out_specs=P(pairs, "y", None),
        check_vma=False,
    )
```

```python
import jax
import jax.numpy as jnp
from jax import lax
from jax.experimental import pallas as pl
from jax.experimental.pallas import tpu as pltpu
from jax.sharding import Mesh
from jax.sharding import PartitionSpec as P

TILES = 8
CAP = 4
NP = TILES * (TILES + 1) // 2
BF = jnp.bfloat16
F32 = jnp.float32
FIRST, SECOND = 16, 20
NEAR = 9
MIB = 1 << 20


def shift(a, axis, d):
    return lax.ppermute(a, axis, [(i, (i + d) % 4) for i in range(4)])


def tie(*arrays):
    return lax.optimization_barrier(arrays)


EARLY_L = [(dc, dz) for dc in range(2) for dz in (0, 1, 3)]
ORDER = [(0, 0), (0, 1), (1, 2), (0, 2), (0, 3), (1, 0), (1, 1), (1, 3)]
SPLIT, END = 80, 160


def place_of(half, k):
    at = 0
    for n, key in enumerate(ORDER):
        at = jnp.where((half == key[0]) & (k == key[1]), 32 * n, at)
    return pl.multiple_of(at, 32)


def product(lefts, rights):
    return lax.dot_general(
        jnp.concatenate(lefts, 0),
        jnp.concatenate(rights, 0),
        (((1,), (1,)), ((), ())),
        preferred_element_type=F32,
    )


def store(meta, sums, out, jp, blocks):
    x, z, c, y = meta[0], meta[1], meta[2], meta[3]
    for n, (dc, dz, half, k) in enumerate(blocks):
        zz, cc = (z + dz) % 4, (c + dc) % 2
        i = 2 * ((x + k) % 4) + zz // 2
        dy = (2 * (zz % 2) + cc - y + 4) % 4
        row = pl.multiple_of((zz // 2 + half) % 2 * 32, 32)
        for b in range(2):
            j = 2 * jp + (z // 2 + b) % 2
            at = jnp.where(i <= j, j * (j + 1) // 2 + i, NP)
            sums[dy, at, pl.ds(row, 32)] = out[32 * n : 32 * n + 32, 128 * b : 128 * b + 128]


def pack(sums, dy, order, first, size, ref, at=0):
    for p in range(size):
        ref[at + p] = sums[dy, order[first + p]].astype(BF)


def early_kernel(meta, order, *refs):
    lefts, rights, outs, sums = refs[:6], refs[6:9], refs[9:10], refs[10]
    x = meta[0]
    for n, dx in enumerate((0, 1, 3)):
        jp = (x + dx) % 4

        def step(k, _):
            @pl.when((x + k) % 4 <= jp)
            def _():
                rows = [ref[pl.ds(place_of(h, k), 32)] for ref in lefts for h in range(2)]
                out = product(rows, [rights[n][...]])
                store(meta, sums, out, jp, [(*key, h, k) for key in EARLY_L for h in range(2)])

            return 0

        lax.fori_loop(0, 4, step, 0)
    pack(sums, 2, order, 0, NEAR, outs[0])


def middle_kernel(meta, order, *refs):
    lefts, far, outs, sums = refs[:6], refs[6:8], refs[9:11], refs[11]
    x = meta[0]
    jp = (x + 2) % 4

    def step(k, _):
        @pl.when((x + k) % 4 <= jp)
        def _():
            rows = [ref[pl.ds(place_of(h, k), 32)] for ref in lefts for h in range(2)]
            out = product(rows, [ref[...] for ref in far])
            store(meta, sums, out, jp, [(*key, h, k) for key in EARLY_L for h in range(2)])

        return 0

    lax.fori_loop(0, 4, step, 0)
    pack(sums, 1, order, 0, FIRST, outs[0])
    pack(sums, 3, order, 0, FIRST, outs[1])


def late_kernel(meta, order1, order2, *refs):
    lates, outs, sums = refs[:2], refs[8:11], refs[11]
    rights = [refs[2:3], refs[3:4], refs[5:7], refs[4:5]]
    keys = [(dc, 2, h, k) for dc in range(2) for h, k in ORDER]
    for dx, right in enumerate(rights):
        out = product([ref[...] for ref in lates], [ref[...] for ref in right])
        store(meta, sums, out, (meta[0] + dx) % 4, keys)
    pack(sums, 1, order2, 0, SECOND, outs[0])
    pack(sums, 2, order1, NEAR, FIRST - NEAR, outs[1])
    pack(sums, 2, order2, 0, SECOND, outs[1], FIRST - NEAR)
    pack(sums, 3, order2, 0, SECOND, outs[2])


def derive_kernel(meta, weights, *refs):
    out = refs[3]
    k, width = weights.shape[1], out.shape[1]
    edge = k // 128 * 128
    out[:, edge:] = jnp.zeros((out.shape[0], width - edge), BF)
    row = pl.multiple_of(128 + meta[0] * 32, 32)
    for n, ref in enumerate(refs[:3]):
        part = ref[pl.ds(row, 32), :k].astype(F32) * weights[...]
        out[32 * n : 32 * n + 32, :k] = part.astype(BF)


def derive(meta, weights, rights):
    smem = pl.BlockSpec(memory_space=pltpu.SMEM)
    vmem = pl.BlockSpec(memory_space=pltpu.VMEM)
    return pl.pallas_call(
        derive_kernel,
        out_shape=jax.ShapeDtypeStruct((96, rights[0].shape[1]), BF),
        in_specs=[smem] + [vmem] * 4,
        out_specs=vmem,
        compiler_params=pltpu.CompilerParams(vmem_limit_bytes=16 * MIB),
        name="derive",
    )(meta, weights, *rights)


def grams(kernel, name, scalars, given, sums=None, parts=()):
    width = given[0].shape[-1]
    smem = pl.BlockSpec(memory_space=pltpu.SMEM)
    vmem = pl.BlockSpec(memory_space=pltpu.VMEM)
    shapes = [jax.ShapeDtypeStruct((n, 64, 128), BF) for n in parts]
    shapes += [jax.ShapeDtypeStruct((4, NP + 1, 64, 128), F32)]
    aliases = {}
    if sums is not None:
        given = [*given, sums]
        aliases = {len(scalars) + len(given) - 1: len(shapes) - 1}
    return pl.pallas_call(
        kernel,
        out_shape=shapes,
        in_specs=[smem] * len(scalars) + [vmem] * len(given),
        out_specs=[vmem] * len(shapes),
        input_output_aliases=aliases,
        compiler_params=pltpu.CompilerParams(vmem_limit_bytes=16 * MIB),
        cost_estimate=pl.CostEstimate(
            flops=2 * 4 * 512 * 256 * width, bytes_accessed=MIB, transcendentals=0
        ),
        name=name,
    )(*scalars, *given)


def prepare_kernel(meta, dens, weights, keep, send, *parts):
    k, width = dens.shape[1], keep.shape[1]
    x, z1 = meta[0], meta[1] // 2
    edge = k // 128 * 128
    for ref in (keep, send):
        ref[:, edge:] = jnp.zeros((128, width - edge), BF)
    keep[:, :k] = dens[pl.ds(pl.multiple_of(z1 * 128, 128), 128), :]
    send[:, :k] = dens[pl.ds(pl.multiple_of((1 - z1) * 128, 128), 128), :]
    for d, ref in enumerate(parts):
        ref[:, edge:] = jnp.zeros((64, width - edge), BF)
        for h in range(2):
            row = pl.multiple_of((z1 + h) % 2 * 128 + (x + d) % 4 * 32, 32)
            part = dens[pl.ds(row, 32), :].astype(F32) * weights[...]
            ref[32 * h : 32 * h + 32, :k] = part.astype(BF)


def prepare(meta, dens, weights, width):
    smem = pl.BlockSpec(memory_space=pltpu.SMEM)
    vmem = pl.BlockSpec(memory_space=pltpu.VMEM)
    shapes = [jax.ShapeDtypeStruct((128, width), BF)] * 2
    shapes += [jax.ShapeDtypeStruct((64, width), BF)] * 4
    return pl.pallas_call(
        prepare_kernel,
        out_shape=shapes,
        in_specs=[smem, vmem, vmem],
        out_specs=[vmem] * 6,
        compiler_params=pltpu.CompilerParams(vmem_limit_bytes=16 * MIB),
        name="prepare",
    )(meta, dens, weights)


def route_kernel(index, order1, order2, sums, *refs):
    near2, one1, one3, two1, two2, two3, out, total = refs
    for p in range(FIRST):
        at = order1[p]
        opposite = near2[p] if p < NEAR else two2[p - NEAR]
        value = sums[0, at] + one1[p].astype(F32) + opposite.astype(F32)
        total[at] = (value + one3[p].astype(F32)).astype(BF)
    for p in range(SECOND):
        at = order2[p]
        value = sums[0, at] + two1[p].astype(F32) + two2[FIRST - NEAR + p].astype(F32)
        total[at] = (value + two3[p].astype(F32)).astype(BF)
    total[NP] = jnp.zeros(total.shape[1:], BF)

    def some(k, _):
        for n in range(8):
            out[8 * k + n] = total[index[8 * k + n]]
        return 0

    lax.fori_loop(0, out.shape[0] // 8, some, 0)


def route(scalars, sums, parts):
    smem = pl.BlockSpec(memory_space=pltpu.SMEM)
    vmem = pl.BlockSpec(memory_space=pltpu.VMEM)
    return pl.pallas_call(
        route_kernel,
        out_shape=jax.ShapeDtypeStruct((scalars[0].shape[0], 64, 128), BF),
        in_specs=[smem] * 3 + [vmem] * 7,
        out_specs=vmem,
        scratch_shapes=[pltpu.VMEM((NP + 1, 64, 128), BF)],
        compiler_params=pltpu.CompilerParams(vmem_limit_bytes=16 * MIB),
        name="route",
    )(*scalars, sums, *parts)


def plan_kernel(meta, first, second, owner, index, order1, order2, count):
    def clear(k, _):
        index[k] = NP
        return 0

    def reset(k, _):
        count[k] = 0
        order1[lax.rem(k, FIRST + 1)] = NP
        order2[lax.rem(k, SECOND + 1)] = NP
        return 0

    def entry(e, _):
        who = owner[e]
        rank = count[who]
        count[who] = rank + 1
        j = second[e]
        index[who * CAP + rank] = j * (j + 1) // 2 + first[e]
        return 0

    lax.fori_loop(0, index.shape[0], clear, 0)
    lax.fori_loop(0, count.shape[0], reset, 0)
    lax.fori_loop(0, owner.shape[0], entry, 0)
    far, z1 = (meta[0] + 2) % 4, meta[1] // 2
    n0, n1, n2 = jnp.int32(0), jnp.int32(NEAR), jnp.int32(0)
    for j in range(TILES):
        for i in range(j + 1):
            mine = z1 == i % 2
            zero = jnp.where(mine & (far != j // 2) & (n0 < NEAR), 1, 0)
            one = jnp.where(mine & (zero == 0) & (n1 < FIRST), 1, 0)
            at = jnp.where(zero == 1, n0, jnp.where(one == 1, n1, FIRST))
            order1[at] = j * (j + 1) // 2 + i
            order2[jnp.where(zero + one == 1, SECOND, n2)] = j * (j + 1) // 2 + i
            n0, n1, n2 = n0 + zero, n1 + one, n2 + 1 - zero - one


def plan(meta, pair_list, owner, slots):
    smem = pl.BlockSpec(memory_space=pltpu.SMEM)
    return pl.pallas_call(
        plan_kernel,
        out_shape=[jax.ShapeDtypeStruct((n,), jnp.int32) for n in (slots, FIRST + 1, SECOND + 1)],
        in_specs=[smem] * 4,
        out_specs=[smem] * 3,
        scratch_shapes=[pltpu.SMEM((slots // CAP,), jnp.int32)],
        compiler_params=pltpu.CompilerParams(vmem_limit_bytes=MIB),
        name="plan",
    )(meta, pair_list[:, 0], pair_list[:, 1], owner[:, 0])


def place_kernel(got, out, blocks, rows, came, went):
    ins = [pltpu.make_async_copy(got.at[:, s], blocks.at[s], came.at[s]) for s in range(CAP)]
    outs = [pltpu.make_async_copy(rows.at[s], out.at[s], went.at[s]) for s in range(CAP)]
    for copy in ins:
        copy.start()
    for s in range(CAP):
        ins[s].wait()
        for src in range(32):
            x, z1, z0, c = src // 8, (src // 4) % 2, (src // 2) % 2, src % 2
            col = (4 * z0 + 2 * c + z1) * 128
            for h in range(2):
                row = h * 128 + x * 32
                part = blocks[s, src, 32 * h : 32 * h + 32]
                rows[s, row : row + 32, col : col + 128] = part.astype(F32)
        outs[s].start()
    for copy in outs:
        copy.wait()


def place(got):
    any_ = pl.BlockSpec(memory_space=pl.ANY)
    return pl.pallas_call(
        place_kernel,
        out_shape=jax.ShapeDtypeStruct((CAP, 256, 1024), F32),
        in_specs=[any_],
        out_specs=any_,
        scratch_shapes=[
            pltpu.VMEM((CAP, 32, 64, 128), BF),
            pltpu.VMEM((CAP, 256, 1024), F32),
            pltpu.SemaphoreType.DMA((CAP,)),
            pltpu.SemaphoreType.DMA((CAP,)),
        ],
        compiler_params=pltpu.CompilerParams(vmem_limit_bytes=16 * MIB),
        name="place",
    )(got)


def on_device(densities, coulomb, pair_list, owner):
    x, z, c, y = (lax.axis_index(n) for n in ("x", "z", "c", "y"))
    k = densities.shape[1]
    meta = jnp.stack([x, z, c, y]).astype(jnp.int32)
    weights = coulomb[None, :]
    keep, send, *mine = prepare(meta, densities, weights, -(-k // 128) * 128)
    got = shift(send, "z", 2)
    other = [(0, 1), (1, 0)]
    got, e1, e2, e3 = tie(
        got, shift(mine[3], "x", 3), shift(mine[2], "x", 2), shift(mine[1], "x", 1)
    )
    right = jnp.concatenate([keep, got], 0)
    pieces = [mine[0], e1, e2, e3]
    left = jnp.concatenate([pieces[k][32 * h : 32 * h + 32] for h, k in ORDER], 0)
    right, left = tie(right, left)

    left3, left1 = shift(left, "z", 1), shift(left, "z", -1)
    right3, right1 = shift(right, "x", 1), shift(right, "x", -1)
    swap0 = lax.ppermute(left, "c", other)
    right3, right1 = tie(right3, right1)

    right2a, right2b = shift(right3[:128], "x", 1), shift(right1[128:], "x", -1)
    late_a, late_b = shift(left3[:SPLIT], "z", 1), shift(left1[SPLIT:END], "z", -1)
    index, order1, order2 = plan(meta, pair_list, owner, 32 * CAP)
    index, near1, near3 = tie(index, left1, left3)
    swap1, swap3 = lax.ppermute(near1, "c", other), lax.ppermute(near3, "c", other)
    lefts = [left, left1, left3, swap0, swap1, swap3]
    rights = [right, right1, right3]

    held = derive(meta, weights, rights)
    order1, held = tie(order1, held)
    first, second = [meta, order1], [meta, order1, order2]
    near, sums = grams(early_kernel, "early", first, lefts + rights, parts=[NEAR])
    near = shift(near, "y", 2)
    late_a, late_b, right2a, right2b, sums, near = tie(late_a, late_b, right2a, right2b, sums, near)
    left2 = jnp.concatenate([late_a, late_b, held], 0)
    swap2 = lax.ppermute(left2, "c", other)
    far = [right2a, right2b]
    one1, one3, sums = grams(middle_kernel, "middle", first, lefts + far, sums, [FIRST] * 2)
    one1, one3 = shift(one1, "y", 1), shift(one3, "y", 3)
    late = [left2, swap2]
    sizes = [SECOND, FIRST - NEAR + SECOND, SECOND]
    *two, sums = grams(late_kernel, "late", second, late + rights + far, sums, sizes)
    two[2], one1, one3 = tie(two[2], one1, one3)
    two = [shift(block, "y", k + 1) for k, block in enumerate(two)]

    routed = route([index, order1, order2], sums, [near, one1, one3, *two]).reshape(32, CAP, 64, 128)
    arrived = lax.all_to_all(routed, ("x", "z", "c"), 0, 0, tiled=True)
    return place(arrived)


def solution(mesh):
    grid = Mesh(mesh.devices.reshape(4, 4, 2, 4), ("x", "z", "c", "y"))
    pairs = ("x", "z", "c")
    return jax.shard_map(
        on_device,
        mesh=grid,
        in_specs=(P(pairs, "y"), P("y"), P(), P()),
        out_specs=P(pairs, "y", None),
        check_vma=False,
    )
```

```python
import jax
import jax.numpy as jnp
from jax import lax
from jax.experimental import pallas as pl
from jax.experimental.pallas import tpu as pltpu
from jax.sharding import Mesh
from jax.sharding import PartitionSpec as P

TILES = 8
CAP = 4
NP = TILES * (TILES + 1) // 2
BF = jnp.bfloat16
F32 = jnp.float32
FIRST, SECOND = 16, 20
NEAR = 9
MIB = 1 << 20


def shift(a, axis, d):
    return lax.ppermute(a, axis, [(i, (i + d) % 4) for i in range(4)])


def tie(*arrays):
    return lax.optimization_barrier(arrays)


EARLY_L = [(dc, dz) for dc in range(2) for dz in (0, 1, 3)]
ORDER = [(0, 0), (0, 1), (1, 2), (0, 2), (0, 3), (1, 0), (1, 1), (1, 3)]
SPLIT, END = 80, 160


def place_of(half, k):
    at = 0
    for n, key in enumerate(ORDER):
        at = jnp.where((half == key[0]) & (k == key[1]), 32 * n, at)
    return pl.multiple_of(at, 32)


def product(lefts, rights):
    return lax.dot_general(
        jnp.concatenate(lefts, 0),
        jnp.concatenate(rights, 0),
        (((1,), (1,)), ((), ())),
        preferred_element_type=F32,
    )


def store(meta, sums, out, jp, blocks):
    x, z, c, y = meta[0], meta[1], meta[2], meta[3]
    for n, (dc, dz, half, k) in enumerate(blocks):
        zz, cc = (z + dz) % 4, (c + dc) % 2
        i = 2 * ((x + k) % 4) + zz // 2
        dy = (2 * (zz % 2) + cc - y + 4) % 4
        row = pl.multiple_of((zz // 2 + half) % 2 * 32, 32)
        for b in range(2):
            j = 2 * jp + (z // 2 + b) % 2
            at = jnp.where(i <= j, j * (j + 1) // 2 + i, NP)
            sums[dy, at, pl.ds(row, 32)] = out[32 * n : 32 * n + 32, 128 * b : 128 * b + 128]


def pack(sums, dy, order, first, size, ref, at=0):
    for p in range(size):
        ref[at + p] = sums[dy, order[first + p]].astype(BF)


def early_kernel(meta, order, *refs):
    lefts, rights, outs, sums = refs[:6], refs[6:9], refs[9:10], refs[10]
    x = meta[0]
    for n, dx in enumerate((0, 1, 3)):
        jp = (x + dx) % 4

        def step(k, _):
            @pl.when((x + k) % 4 <= jp)
            def _():
                rows = [ref[pl.ds(place_of(h, k), 32)] for ref in lefts for h in range(2)]
                out = product(rows, [rights[n][...]])
                store(meta, sums, out, jp, [(*key, h, k) for key in EARLY_L for h in range(2)])

            return 0

        lax.fori_loop(0, 4, step, 0)
    pack(sums, 2, order, 0, NEAR, outs[0])


def middle_kernel(meta, order, *refs):
    lefts, far, outs, sums = refs[:6], refs[6:8], refs[9:11], refs[11]
    x = meta[0]
    jp = (x + 2) % 4

    def step(k, _):
        @pl.when((x + k) % 4 <= jp)
        def _():
            rows = [ref[pl.ds(place_of(h, k), 32)] for ref in lefts for h in range(2)]
            out = product(rows, [ref[...] for ref in far])
            store(meta, sums, out, jp, [(*key, h, k) for key in EARLY_L for h in range(2)])

        return 0

    lax.fori_loop(0, 4, step, 0)
    pack(sums, 1, order, 0, FIRST, outs[0])
    pack(sums, 3, order, 0, FIRST, outs[1])


def late_kernel(meta, order1, order2, *refs):
    lates, outs, sums = refs[:2], refs[8:11], refs[11]
    rights = [refs[2:3], refs[3:4], refs[5:7], refs[4:5]]
    keys = [(dc, 2, h, k) for dc in range(2) for h, k in ORDER]
    for dx, right in enumerate(rights):
        out = product([ref[...] for ref in lates], [ref[...] for ref in right])
        store(meta, sums, out, (meta[0] + dx) % 4, keys)
    pack(sums, 1, order2, 0, SECOND, outs[0])
    pack(sums, 2, order1, NEAR, FIRST - NEAR, outs[1])
    pack(sums, 2, order2, 0, SECOND, outs[1], FIRST - NEAR)
    pack(sums, 3, order2, 0, SECOND, outs[2])


def derive_kernel(meta, weights, *refs):
    out = refs[3]
    k, width = weights.shape[1], out.shape[1]
    edge = k // 128 * 128
    out[:, edge:] = jnp.zeros((out.shape[0], width - edge), BF)
    row = pl.multiple_of(128 + meta[0] * 32, 32)
    for n, ref in enumerate(refs[:3]):
        part = ref[pl.ds(row, 32), :k].astype(F32) * weights[...]
        out[32 * n : 32 * n + 32, :k] = part.astype(BF)


def derive(meta, weights, rights):
    smem = pl.BlockSpec(memory_space=pltpu.SMEM)
    vmem = pl.BlockSpec(memory_space=pltpu.VMEM)
    return pl.pallas_call(
        derive_kernel,
        out_shape=jax.ShapeDtypeStruct((96, rights[0].shape[1]), BF),
        in_specs=[smem] + [vmem] * 4,
        out_specs=vmem,
        compiler_params=pltpu.CompilerParams(vmem_limit_bytes=16 * MIB),
        name="derive",
    )(meta, weights, *rights)


def grams(kernel, name, scalars, given, sums=None, parts=()):
    width = given[0].shape[-1]
    smem = pl.BlockSpec(memory_space=pltpu.SMEM)
    vmem = pl.BlockSpec(memory_space=pltpu.VMEM)
    shapes = [jax.ShapeDtypeStruct((n, 64, 128), BF) for n in parts]
    shapes += [jax.ShapeDtypeStruct((4, NP + 1, 64, 128), F32)]
    aliases = {}
    if sums is not None:
        given = [*given, sums]
        aliases = {len(scalars) + len(given) - 1: len(shapes) - 1}
    return pl.pallas_call(
        kernel,
        out_shape=shapes,
        in_specs=[smem] * len(scalars) + [vmem] * len(given),
        out_specs=[vmem] * len(shapes),
        input_output_aliases=aliases,
        compiler_params=pltpu.CompilerParams(vmem_limit_bytes=16 * MIB),
        cost_estimate=pl.CostEstimate(
            flops=2 * 4 * 512 * 256 * width, bytes_accessed=MIB, transcendentals=0
        ),
        name=name,
    )(*scalars, *given)


def prepare_kernel(meta, dens, weights, keep, send, *parts):
    k, width = dens.shape[1], keep.shape[1]
    x, z1 = meta[0], meta[1] // 2
    edge = k // 128 * 128
    for ref in (keep, send):
        ref[:, edge:] = jnp.zeros((128, width - edge), BF)
    keep[:, :k] = dens[pl.ds(pl.multiple_of(z1 * 128, 128), 128), :]
    send[:, :k] = dens[pl.ds(pl.multiple_of((1 - z1) * 128, 128), 128), :]
    for d, ref in enumerate(parts):
        ref[:, edge:] = jnp.zeros((64, width - edge), BF)
        for h in range(2):
            row = pl.multiple_of((z1 + h) % 2 * 128 + (x + d) % 4 * 32, 32)
            part = dens[pl.ds(row, 32), :].astype(F32) * weights[...]
            ref[32 * h : 32 * h + 32, :k] = part.astype(BF)


def prepare(meta, dens, weights, width):
    smem = pl.BlockSpec(memory_space=pltpu.SMEM)
    vmem = pl.BlockSpec(memory_space=pltpu.VMEM)
    shapes = [jax.ShapeDtypeStruct((128, width), BF)] * 2
    shapes += [jax.ShapeDtypeStruct((64, width), BF)] * 4
    return pl.pallas_call(
        prepare_kernel,
        out_shape=shapes,
        in_specs=[smem, vmem, vmem],
        out_specs=[vmem] * 6,
        compiler_params=pltpu.CompilerParams(vmem_limit_bytes=16 * MIB),
        name="prepare",
    )(meta, dens, weights)


def route_kernel(index, order1, order2, sums, *refs):
    near2, one1, one3, two1, two2, two3, out, total = refs
    for p in range(FIRST):
        at = order1[p]
        opposite = near2[p] if p < NEAR else two2[p - NEAR]
        value = sums[0, at] + one1[p].astype(F32) + opposite.astype(F32)
        total[at] = (value + one3[p].astype(F32)).astype(BF)
    for p in range(SECOND):
        at = order2[p]
        value = sums[0, at] + two1[p].astype(F32) + two2[FIRST - NEAR + p].astype(F32)
        total[at] = (value + two3[p].astype(F32)).astype(BF)
    total[NP] = jnp.zeros(total.shape[1:], BF)

    def some(k, _):
        for n in range(8):
            out[8 * k + n] = total[index[8 * k + n]]
        return 0

    lax.fori_loop(0, out.shape[0] // 8, some, 0)


def route(scalars, sums, parts):
    smem = pl.BlockSpec(memory_space=pltpu.SMEM)
    vmem = pl.BlockSpec(memory_space=pltpu.VMEM)
    return pl.pallas_call(
        route_kernel,
        out_shape=jax.ShapeDtypeStruct((scalars[0].shape[0], 64, 128), BF),
        in_specs=[smem] * 3 + [vmem] * 7,
        out_specs=vmem,
        scratch_shapes=[pltpu.VMEM((NP + 1, 64, 128), BF)],
        compiler_params=pltpu.CompilerParams(vmem_limit_bytes=16 * MIB),
        name="route",
    )(*scalars, sums, *parts)


def plan_kernel(meta, first, second, owner, index, order1, order2, count):
    def clear(k, _):
        index[k] = NP
        return 0

    def reset(k, _):
        count[k] = 0
        order1[lax.rem(k, FIRST + 1)] = NP
        order2[lax.rem(k, SECOND + 1)] = NP
        return 0

    def entry(e, _):
        who = owner[e]
        rank = count[who]
        count[who] = rank + 1
        j = second[e]
        index[who * CAP + rank] = j * (j + 1) // 2 + first[e]
        return 0

    lax.fori_loop(0, index.shape[0], clear, 0)
    lax.fori_loop(0, count.shape[0], reset, 0)
    lax.fori_loop(0, owner.shape[0], entry, 0)
    far, z1 = (meta[0] + 2) % 4, meta[1] // 2
    n0, n1, n2 = jnp.int32(0), jnp.int32(NEAR), jnp.int32(0)
    for j in range(TILES):
        for i in range(j + 1):
            mine = z1 == i % 2
            zero = jnp.where(mine & (far != j // 2) & (n0 < NEAR), 1, 0)
            one = jnp.where(mine & (zero == 0) & (n1 < FIRST), 1, 0)
            at = jnp.where(zero == 1, n0, jnp.where(one == 1, n1, FIRST))
            order1[at] = j * (j + 1) // 2 + i
            order2[jnp.where(zero + one == 1, SECOND, n2)] = j * (j + 1) // 2 + i
            n0, n1, n2 = n0 + zero, n1 + one, n2 + 1 - zero - one


def plan(meta, pair_list, owner, slots):
    smem = pl.BlockSpec(memory_space=pltpu.SMEM)
    return pl.pallas_call(
        plan_kernel,
        out_shape=[jax.ShapeDtypeStruct((n,), jnp.int32) for n in (slots, FIRST + 1, SECOND + 1)],
        in_specs=[smem] * 4,
        out_specs=[smem] * 3,
        scratch_shapes=[pltpu.SMEM((slots // CAP,), jnp.int32)],
        compiler_params=pltpu.CompilerParams(vmem_limit_bytes=MIB),
        name="plan",
    )(meta, pair_list[:, 0], pair_list[:, 1], owner[:, 0])


def place_kernel(got, out, blocks, rows, came, went):
    ins = [pltpu.make_async_copy(got.at[:, s], blocks.at[s], came.at[s]) for s in range(CAP)]
    outs = [pltpu.make_async_copy(rows.at[s], out.at[s], went.at[s]) for s in range(CAP)]
    for copy in ins:
        copy.start()
    for s in range(CAP):
        ins[s].wait()
        for src in range(32):
            x, z1, z0, c = src // 8, (src // 4) % 2, (src // 2) % 2, src % 2
            col = (4 * z0 + 2 * c + z1) * 128
            for h in range(2):
                row = h * 128 + x * 32
                part = blocks[s, src, 32 * h : 32 * h + 32]
                rows[s, row : row + 32, col : col + 128] = part.astype(F32)
        outs[s].start()
    for copy in outs:
        copy.wait()


def place(got):
    any_ = pl.BlockSpec(memory_space=pl.ANY)
    return pl.pallas_call(
        place_kernel,
        out_shape=jax.ShapeDtypeStruct((CAP, 256, 1024), F32),
        in_specs=[any_],
        out_specs=any_,
        scratch_shapes=[
            pltpu.VMEM((CAP, 32, 64, 128), BF),
            pltpu.VMEM((CAP, 256, 1024), F32),
            pltpu.SemaphoreType.DMA((CAP,)),
            pltpu.SemaphoreType.DMA((CAP,)),
        ],
        compiler_params=pltpu.CompilerParams(vmem_limit_bytes=16 * MIB),
        name="place",
    )(got)


def on_device(densities, coulomb, pair_list, owner):
    x, z, c, y = (lax.axis_index(n) for n in ("x", "z", "c", "y"))
    k = densities.shape[1]
    meta = jnp.stack([x, z, c, y]).astype(jnp.int32)
    weights = coulomb[None, :]
    keep, send, *mine = prepare(meta, densities, weights, -(-k // 128) * 128)
    got = shift(send, "z", 2)
    other = [(0, 1), (1, 0)]
    e1, e2, e3 = shift(mine[3], "x", 3), shift(mine[2], "x", 2), shift(mine[1], "x", 1)
    right = jnp.concatenate([keep, got], 0)
    pieces = [mine[0], e1, e2, e3]
    left = jnp.concatenate([pieces[k][32 * h : 32 * h + 32] for h, k in ORDER], 0)
    right, left = tie(right, left)

    left3, left1 = shift(left, "z", 1), shift(left, "z", -1)
    right3, right1 = shift(right, "x", 1), shift(right, "x", -1)
    swap0 = lax.ppermute(left, "c", other)
    right3, right1 = tie(right3, right1)

    right2a, right2b = shift(right3[:128], "x", 1), shift(right1[128:], "x", -1)
    late_a, late_b = shift(left3[:SPLIT], "z", 1), shift(left1[SPLIT:END], "z", -1)
    index, order1, order2 = plan(meta, pair_list, owner, 32 * CAP)
    index, near1, near3 = tie(index, left1, left3)
    swap1, swap3 = lax.ppermute(near1, "c", other), lax.ppermute(near3, "c", other)
    lefts = [left, left1, left3, swap0, swap1, swap3]
    rights = [right, right1, right3]

    held = derive(meta, weights, rights)
    first, second = [meta, order1], [meta, order1, order2]
    near, sums = grams(early_kernel, "early", first, lefts + rights, parts=[NEAR])
    near = shift(near, "y", 2)
    late_a, late_b, right2a, right2b, sums, near = tie(late_a, late_b, right2a, right2b, sums, near)
    left2 = jnp.concatenate([late_a, late_b, held], 0)
    swap2 = lax.ppermute(left2, "c", other)
    far = [right2a, right2b]
    one1, one3, sums = grams(middle_kernel, "middle", first, lefts + far, sums, [FIRST] * 2)
    one1, one3 = shift(one1, "y", 1), shift(one3, "y", 3)
    late = [left2, swap2]
    sizes = [SECOND, FIRST - NEAR + SECOND, SECOND]
    *two, sums = grams(late_kernel, "late", second, late + rights + far, sums, sizes)
    two[2], one1, one3 = tie(two[2], one1, one3)
    two = [shift(block, "y", k + 1) for k, block in enumerate(two)]

    routed = route([index, order1, order2], sums, [near, one1, one3, *two]).reshape(32, CAP, 64, 128)
    arrived = lax.all_to_all(routed, ("x", "z", "c"), 0, 0, tiled=True)
    return place(arrived)


def solution(mesh):
    grid = Mesh(mesh.devices.reshape(4, 4, 2, 4), ("x", "z", "c", "y"))
    pairs = ("x", "z", "c")
    return jax.shard_map(
        on_device,
        mesh=grid,
        in_specs=(P(pairs, "y"), P("y"), P(), P()),
        out_specs=P(pairs, "y", None),
        check_vma=False,
    )
```

```python
import jax
import jax.numpy as jnp
from jax import lax
from jax.experimental import pallas as pl
from jax.experimental.pallas import tpu as pltpu
from jax.sharding import Mesh
from jax.sharding import PartitionSpec as P

TILES = 8
CAP = 4
NP = TILES * (TILES + 1) // 2
BF = jnp.bfloat16
F32 = jnp.float32
FIRST, SECOND = 16, 20
NEAR = 9
MIB = 1 << 20


def shift(a, axis, d):
    return lax.ppermute(a, axis, [(i, (i + d) % 4) for i in range(4)])


def tie(*arrays):
    return lax.optimization_barrier(arrays)


EARLY_L = [(dc, dz) for dc in range(2) for dz in (0, 1, 3)]
ORDER = [(0, 0), (0, 1), (1, 2), (0, 2), (0, 3), (1, 0), (1, 1), (1, 3)]
SPLIT, END = 80, 160


def place_of(half, k):
    at = 0
    for n, key in enumerate(ORDER):
        at = jnp.where((half == key[0]) & (k == key[1]), 32 * n, at)
    return pl.multiple_of(at, 32)


def product(lefts, rights):
    return lax.dot_general(
        jnp.concatenate(lefts, 0),
        jnp.concatenate(rights, 0),
        (((1,), (1,)), ((), ())),
        preferred_element_type=F32,
    )


def store(meta, sums, out, jp, blocks):
    x, z, c, y = meta[0], meta[1], meta[2], meta[3]
    for n, (dc, dz, half, k) in enumerate(blocks):
        zz, cc = (z + dz) % 4, (c + dc) % 2
        i = 2 * ((x + k) % 4) + zz // 2
        dy = (2 * (zz % 2) + cc - y + 4) % 4
        row = pl.multiple_of((zz // 2 + half) % 2 * 32, 32)
        for b in range(2):
            j = 2 * jp + (z // 2 + b) % 2
            at = jnp.where(i <= j, j * (j + 1) // 2 + i, NP)
            sums[dy, at, pl.ds(row, 32)] = out[32 * n : 32 * n + 32, 128 * b : 128 * b + 128]


def pack(sums, dy, order, first, size, ref, at=0):
    for p in range(size):
        ref[at + p] = sums[dy, order[first + p]].astype(BF)


def early_kernel(meta, order, *refs):
    lefts, rights, outs, sums = refs[:6], refs[6:9], refs[9:10], refs[10]
    x = meta[0]
    for n, dx in enumerate((0, 1, 3)):
        jp = (x + dx) % 4

        def step(k, _):
            @pl.when((x + k) % 4 <= jp)
            def _():
                rows = [ref[pl.ds(place_of(h, k), 32)] for ref in lefts for h in range(2)]
                out = product(rows, [rights[n][...]])
                store(meta, sums, out, jp, [(*key, h, k) for key in EARLY_L for h in range(2)])

            return 0

        lax.fori_loop(0, 4, step, 0)
    pack(sums, 2, order, 0, NEAR, outs[0])


def middle_kernel(meta, order, *refs):
    lefts, far, outs, sums = refs[:6], refs[6:8], refs[9:11], refs[11]
    x = meta[0]
    jp = (x + 2) % 4

    def step(k, _):
        @pl.when((x + k) % 4 <= jp)
        def _():
            rows = [ref[pl.ds(place_of(h, k), 32)] for ref in lefts for h in range(2)]
            out = product(rows, [ref[...] for ref in far])
            store(meta, sums, out, jp, [(*key, h, k) for key in EARLY_L for h in range(2)])

        return 0

    lax.fori_loop(0, 4, step, 0)
    pack(sums, 1, order, 0, FIRST, outs[0])
    pack(sums, 3, order, 0, FIRST, outs[1])


def late_kernel(meta, order1, order2, *refs):
    lates, outs, sums = refs[:2], refs[8:11], refs[11]
    rights = [refs[2:3], refs[3:4], refs[5:7], refs[4:5]]
    keys = [(dc, 2, h, k) for dc in range(2) for h, k in ORDER]
    for dx, right in enumerate(rights):
        out = product([ref[...] for ref in lates], [ref[...] for ref in right])
        store(meta, sums, out, (meta[0] + dx) % 4, keys)
    pack(sums, 1, order2, 0, SECOND, outs[0])
    pack(sums, 2, order1, NEAR, FIRST - NEAR, outs[1])
    pack(sums, 2, order2, 0, SECOND, outs[1], FIRST - NEAR)
    pack(sums, 3, order2, 0, SECOND, outs[2])


def derive_kernel(meta, weights, *refs):
    out = refs[3]
    k, width = weights.shape[1], out.shape[1]
    edge = k // 128 * 128
    out[:, edge:] = jnp.zeros((out.shape[0], width - edge), BF)
    row = pl.multiple_of(128 + meta[0] * 32, 32)
    for n, ref in enumerate(refs[:3]):
        part = ref[pl.ds(row, 32), :k].astype(F32) * weights[...]
        out[32 * n : 32 * n + 32, :k] = part.astype(BF)


def derive(meta, weights, rights):
    smem = pl.BlockSpec(memory_space=pltpu.SMEM)
    vmem = pl.BlockSpec(memory_space=pltpu.VMEM)
    return pl.pallas_call(
        derive_kernel,
        out_shape=jax.ShapeDtypeStruct((96, rights[0].shape[1]), BF),
        in_specs=[smem] + [vmem] * 4,
        out_specs=vmem,
        compiler_params=pltpu.CompilerParams(vmem_limit_bytes=16 * MIB),
        name="derive",
    )(meta, weights, *rights)


def grams(kernel, name, scalars, given, sums=None, parts=()):
    width = given[0].shape[-1]
    smem = pl.BlockSpec(memory_space=pltpu.SMEM)
    vmem = pl.BlockSpec(memory_space=pltpu.VMEM)
    shapes = [jax.ShapeDtypeStruct((n, 64, 128), BF) for n in parts]
    shapes += [jax.ShapeDtypeStruct((4, NP + 1, 64, 128), F32)]
    aliases = {}
    if sums is not None:
        given = [*given, sums]
        aliases = {len(scalars) + len(given) - 1: len(shapes) - 1}
    return pl.pallas_call(
        kernel,
        out_shape=shapes,
        in_specs=[smem] * len(scalars) + [vmem] * len(given),
        out_specs=[vmem] * len(shapes),
        input_output_aliases=aliases,
        compiler_params=pltpu.CompilerParams(vmem_limit_bytes=16 * MIB),
        cost_estimate=pl.CostEstimate(
            flops=2 * 4 * 512 * 256 * width, bytes_accessed=MIB, transcendentals=0
        ),
        name=name,
    )(*scalars, *given)


def prepare_kernel(meta, dens, weights, keep, send, *parts):
    k, width = dens.shape[1], keep.shape[1]
    x, z1 = meta[0], meta[1] // 2
    edge = k // 128 * 128
    for ref in (keep, send):
        ref[:, edge:] = jnp.zeros((128, width - edge), BF)
    keep[:, :k] = dens[pl.ds(pl.multiple_of(z1 * 128, 128), 128), :]
    send[:, :k] = dens[pl.ds(pl.multiple_of((1 - z1) * 128, 128), 128), :]
    for d, ref in enumerate(parts):
        ref[:, edge:] = jnp.zeros((64, width - edge), BF)
        for h in range(2):
            row = pl.multiple_of((z1 + h) % 2 * 128 + (x + d) % 4 * 32, 32)
            part = dens[pl.ds(row, 32), :].astype(F32) * weights[...]
            ref[32 * h : 32 * h + 32, :k] = part.astype(BF)


def prepare(meta, dens, weights, width):
    smem = pl.BlockSpec(memory_space=pltpu.SMEM)
    vmem = pl.BlockSpec(memory_space=pltpu.VMEM)
    shapes = [jax.ShapeDtypeStruct((128, width), BF)] * 2
    shapes += [jax.ShapeDtypeStruct((64, width), BF)] * 4
    return pl.pallas_call(
        prepare_kernel,
        out_shape=shapes,
        in_specs=[smem, vmem, vmem],
        out_specs=[vmem] * 6,
        compiler_params=pltpu.CompilerParams(vmem_limit_bytes=16 * MIB),
        name="prepare",
    )(meta, dens, weights)


def route_kernel(index, order1, order2, sums, *refs):
    near2, one1, one3, two1, two2, two3, out, total = refs
    for p in range(FIRST):
        at = order1[p]
        opposite = near2[p] if p < NEAR else two2[p - NEAR]
        value = sums[0, at] + one1[p].astype(F32) + opposite.astype(F32)
        total[at] = (value + one3[p].astype(F32)).astype(BF)
    for p in range(SECOND):
        at = order2[p]
        value = sums[0, at] + two1[p].astype(F32) + two2[FIRST - NEAR + p].astype(F32)
        total[at] = (value + two3[p].astype(F32)).astype(BF)
    total[NP] = jnp.zeros(total.shape[1:], BF)

    def some(k, _):
        for n in range(8):
            out[8 * k + n] = total[index[8 * k + n]]
        return 0

    lax.fori_loop(0, out.shape[0] // 8, some, 0)


def route(scalars, sums, parts):
    smem = pl.BlockSpec(memory_space=pltpu.SMEM)
    vmem = pl.BlockSpec(memory_space=pltpu.VMEM)
    return pl.pallas_call(
        route_kernel,
        out_shape=jax.ShapeDtypeStruct((scalars[0].shape[0], 64, 128), BF),
        in_specs=[smem] * 3 + [vmem] * 7,
        out_specs=vmem,
        scratch_shapes=[pltpu.VMEM((NP + 1, 64, 128), BF)],
        compiler_params=pltpu.CompilerParams(vmem_limit_bytes=16 * MIB),
        name="route",
    )(*scalars, sums, *parts)


def plan_kernel(meta, first, second, owner, index, order1, order2, count):
    def clear(k, _):
        index[k] = NP
        return 0

    def reset(k, _):
        count[k] = 0
        order1[lax.rem(k, FIRST + 1)] = NP
        order2[lax.rem(k, SECOND + 1)] = NP
        return 0

    def entry(e, _):
        who = owner[e]
        rank = count[who]
        count[who] = rank + 1
        j = second[e]
        index[who * CAP + rank] = j * (j + 1) // 2 + first[e]
        return 0

    lax.fori_loop(0, index.shape[0], clear, 0)
    lax.fori_loop(0, count.shape[0], reset, 0)
    lax.fori_loop(0, owner.shape[0], entry, 0)
    far, z1 = (meta[0] + 2) % 4, meta[1] // 2
    n0, n1, n2 = jnp.int32(0), jnp.int32(NEAR), jnp.int32(0)
    for j in range(TILES):
        for i in range(j + 1):
            mine = z1 == i % 2
            zero = jnp.where(mine & (far != j // 2) & (n0 < NEAR), 1, 0)
            one = jnp.where(mine & (zero == 0) & (n1 < FIRST), 1, 0)
            at = jnp.where(zero == 1, n0, jnp.where(one == 1, n1, FIRST))
            order1[at] = j * (j + 1) // 2 + i
            order2[jnp.where(zero + one == 1, SECOND, n2)] = j * (j + 1) // 2 + i
            n0, n1, n2 = n0 + zero, n1 + one, n2 + 1 - zero - one


def plan(meta, pair_list, owner, slots):
    smem = pl.BlockSpec(memory_space=pltpu.SMEM)
    return pl.pallas_call(
        plan_kernel,
        out_shape=[jax.ShapeDtypeStruct((n,), jnp.int32) for n in (slots, FIRST + 1, SECOND + 1)],
        in_specs=[smem] * 4,
        out_specs=[smem] * 3,
        scratch_shapes=[pltpu.SMEM((slots // CAP,), jnp.int32)],
        compiler_params=pltpu.CompilerParams(vmem_limit_bytes=MIB),
        name="plan",
    )(meta, pair_list[:, 0], pair_list[:, 1], owner[:, 0])


def place_kernel(got, out, blocks, rows, came, went):
    ins = [pltpu.make_async_copy(got.at[:, s], blocks.at[s], came.at[s]) for s in range(CAP)]
    outs = [pltpu.make_async_copy(rows.at[s], out.at[s], went.at[s]) for s in range(CAP)]
    for copy in ins:
        copy.start()
    for s in range(CAP):
        ins[s].wait()
        for src in range(32):
            x, z1, z0, c = src // 8, (src // 4) % 2, (src // 2) % 2, src % 2
            col = (4 * z0 + 2 * c + z1) * 128
            for h in range(2):
                row = h * 128 + x * 32
                part = blocks[s, src, 32 * h : 32 * h + 32]
                rows[s, row : row + 32, col : col + 128] = part.astype(F32)
        outs[s].start()
    for copy in outs:
        copy.wait()


def place(got):
    any_ = pl.BlockSpec(memory_space=pl.ANY)
    return pl.pallas_call(
        place_kernel,
        out_shape=jax.ShapeDtypeStruct((CAP, 256, 1024), F32),
        in_specs=[any_],
        out_specs=any_,
        scratch_shapes=[
            pltpu.VMEM((CAP, 32, 64, 128), BF),
            pltpu.VMEM((CAP, 256, 1024), F32),
            pltpu.SemaphoreType.DMA((CAP,)),
            pltpu.SemaphoreType.DMA((CAP,)),
        ],
        compiler_params=pltpu.CompilerParams(vmem_limit_bytes=16 * MIB),
        name="place",
    )(got)


def on_device(densities, coulomb, pair_list, owner):
    x, z, c, y = (lax.axis_index(n) for n in ("x", "z", "c", "y"))
    k = densities.shape[1]
    meta = jnp.stack([x, z, c, y]).astype(jnp.int32)
    weights = coulomb[None, :]
    keep, send, *mine = prepare(meta, densities, weights, -(-k // 128) * 128)
    got = shift(send, "z", 2)
    other = [(0, 1), (1, 0)]
    e1, e2, e3 = shift(mine[3], "x", 3), shift(mine[2], "x", 2), shift(mine[1], "x", 1)
    right = jnp.concatenate([keep, got], 0)
    pieces = [mine[0], e1, e2, e3]
    left = jnp.concatenate([pieces[k][32 * h : 32 * h + 32] for h, k in ORDER], 0)
    right, left = tie(right, left)

    left3, left1 = shift(left, "z", 1), shift(left, "z", -1)
    right3, right1 = shift(right, "x", 1), shift(right, "x", -1)
    swap0 = lax.ppermute(left, "c", other)
    right3, right1 = tie(right3, right1)

    right2a, right2b = shift(right3[:128], "x", 1), shift(right1[128:], "x", -1)
    late_a, late_b = shift(left3[:SPLIT], "z", 1), shift(left1[SPLIT:END], "z", -1)
    index, order1, order2 = plan(meta, pair_list, owner, 32 * CAP)
    index, near3 = tie(index, left3)
    near1 = left1
    swap1, swap3 = lax.ppermute(near1, "c", other), lax.ppermute(near3, "c", other)
    lefts = [left, left1, left3, swap0, swap1, swap3]
    rights = [right, right1, right3]

    held = derive(meta, weights, rights)
    first, second = [meta, order1], [meta, order1, order2]
    near, sums = grams(early_kernel, "early", first, lefts + rights, parts=[NEAR])
    near = shift(near, "y", 2)
    late_a, late_b, right2a, right2b, sums, near = tie(late_a, late_b, right2a, right2b, sums, near)
    left2 = jnp.concatenate([late_a, late_b, held], 0)
    swap2 = lax.ppermute(left2, "c", other)
    far = [right2a, right2b]
    one1, one3, sums = grams(middle_kernel, "middle", first, lefts + far, sums, [FIRST] * 2)
    one1, one3 = shift(one1, "y", 1), shift(one3, "y", 3)
    late = [left2, swap2]
    sizes = [SECOND, FIRST - NEAR + SECOND, SECOND]
    *two, sums = grams(late_kernel, "late", second, late + rights + far, sums, sizes)
    two[2], one1, one3 = tie(two[2], one1, one3)
    two = [shift(block, "y", k + 1) for k, block in enumerate(two)]

    routed = route([index, order1, order2], sums, [near, one1, one3, *two]).reshape(32, CAP, 64, 128)
    arrived = lax.all_to_all(routed, ("x", "z", "c"), 0, 0, tiled=True)
    return place(arrived)


def solution(mesh):
    grid = Mesh(mesh.devices.reshape(4, 4, 2, 4), ("x", "z", "c", "y"))
    pairs = ("x", "z", "c")
    return jax.shard_map(
        on_device,
        mesh=grid,
        in_specs=(P(pairs, "y"), P("y"), P(), P()),
        out_specs=P(pairs, "y", None),
        check_vma=False,
    )
```
